32 devices in a mesh: dp: 4 (over y, x), ctx: 8 (over z, core).
Axes of the slice: x: 2, y: 2, z: 4, core: 2. Of those that a mesh axis runs over, the one named last changes fastest.
Arguments:
- queries: bfloat16 [4, 1024, 4096], P('dp', 'ctx'), may hold values from -5 to 5
- query_tangent: bfloat16 [4, 1024, 4096], P('dp', 'ctx'), may hold values from -6 to 6
- keys: bfloat16 [4, 512, 4096], P('dp', 'ctx'), may hold values from -5 to 5
- key_tangent: bfloat16 [4, 512, 4096], P('dp', 'ctx'), may hold values from -6 to 6
- values: bfloat16 [4, 512, 4096], P('dp', 'ctx'), may hold values from -6 to 6
- value_tangent: bfloat16 [4, 512, 4096], P('dp', 'ctx'), may hold values from -6 to 6
- out_gain: bfloat16 [4096], replicated, may hold values from 0.5 to 2
- grad_y: bfloat16 [4, 1024, 4096], P('dp', 'ctx'), may hold values from -6 to 6
- grad_y_tan: bfloat16 [4, 1024, 4096], P('dp', 'ctx'), may hold values from -6 to 6
Outputs:
- query_gradient: bfloat16 [4, 1024, 4096], P('dp', 'ctx')
- query_tangent_gradient: bfloat16 [4, 1024, 4096], P('dp', 'ctx')
- key_gradient: bfloat16 [4, 512, 4096], P('dp', 'ctx')
- key_tangent_gradient: bfloat16 [4, 512, 4096], P('dp', 'ctx')
- value_gradient: bfloat16 [4, 512, 4096], P('dp', 'ctx')
- value_tangent_gradient: bfloat16 [4, 512, 4096], P('dp', 'ctx')
- gain_grad: float32 [4096], P('ctx')
The draws below stay inside these ranges and needn't reach their ends.
All inputs are finite; a program needn't handle non-finite values.
Results may differ from the reference program's by a relative error of at most 0.0076.
Values may be sent and summed in bfloat16 or wider, within the bound.
No kernel may reach another device: no remote copies, remote signals or barrier semaphores. Data moves between devices by JAX's collectives and lax.ppermute only.
A program may use at most 128 MiB of HBM per device.

```python
import math
import jax
import jax.numpy as jnp
from jax import lax

HEADS = 32
HEAD_DIM = 128
WIDTH = 4096
PROBES = 4
QUERIES = 1024
KEYS = 512


def draw_queries(key, part):
    own_key = jax.random.fold_in(key, 11)
    values_field = jnp.clip(jax.random.normal(own_key, (PROBES, QUERIES, WIDTH), jnp.float32), -5.0, 5.0)
    return values_field.astype(jnp.bfloat16)


def draw_keys(key, part):
    own_key = jax.random.fold_in(key, 23)
    values_field = jnp.clip(jax.random.normal(own_key, (PROBES, KEYS, WIDTH), jnp.float32), -5.0, 5.0)
    return values_field.astype(jnp.bfloat16)


def shard_levels(rng, dims, cuts, smallest, high):
    gain, own = 1.0, jax.random.fold_in(rng, 6)
    for axis_at, parts in cuts:
        steps = jnp.exp(jax.random.uniform(jax.random.fold_in(own, axis_at), (parts,), jnp.float32, smallest / len(cuts), high / len(cuts)))
        gain = gain * jnp.repeat(steps, dims[axis_at] // parts).reshape([-1 if axis == axis_at else 1 for axis in range(len(dims))])
    return gain


def normal_values(rng, extent, scale, reach, shards=(), kind=jnp.bfloat16):
    values = scale * jax.random.normal(rng, extent, jnp.float32)
    if shards:
        values = values * shard_levels(rng, extent, shards, -0.22, 0.18)
    return jnp.clip(values, -reach, reach).astype(kind)


def setup_inputs(seed: int = 0) -> dict:
    key_list = jax.random.split(jax.random.key(seed), 10)
    return {
        "queries": draw_queries(jax.random.fold_in(key_list[9], 71), 0),
        "query_tangent": normal_values(key_list[1], (PROBES, QUERIES, WIDTH), 1.0, 6.0, ((0, 4), (1, 8))),
        "keys": draw_keys(jax.random.fold_in(key_list[9], 71), 0),
        "key_tangent": normal_values(key_list[3], (PROBES, KEYS, WIDTH), 1.0, 6.0, ((0, 4), (1, 8))),
        "values": normal_values(key_list[4], (PROBES, KEYS, WIDTH), 1.0, 6.0, ((0, 4), (1, 8))),
        "value_tangent": normal_values(key_list[5], (PROBES, KEYS, WIDTH), 1.0, 6.0, ((0, 4), (1, 8))),
        "out_gain": jnp.clip(jnp.exp(jax.random.uniform(key_list[6], (WIDTH,), jnp.float32, math.log(0.5), math.log(2.0))), 0.5, 2.0).astype(jnp.bfloat16),
        "grad_y": normal_values(key_list[7], (PROBES, QUERIES, WIDTH), 1.0, 6.0, ((0, 4), (1, 8))),
        "grad_y_tan": normal_values(key_list[8], (PROBES, QUERIES, WIDTH), 1.0, 6.0, ((0, 4), (1, 8))),
    }


def inner_product(pattern, left_op, right_op):
    return jnp.einsum(pattern, left_op.astype(jnp.float32), right_op.astype(jnp.float32))

def reduced_precision(values_in):
    return lax.optimization_barrier(values_in.astype(jnp.bfloat16))

def block_terms(query_block, query_tangents, output_gradient, tangent_gradient, every_key, key_tangents, every_value, value_tangents, scale_factor):
    score_matrix = inner_product('zqc,pqc->qzp', query_block, every_key) * scale_factor
    score_tangent = (inner_product('zqc,pqc->qzp', query_tangents, every_key) + inner_product('zqc,pqc->qzp', query_block, key_tangents)) * scale_factor
    row_max = lax.optimization_barrier(jnp.max(score_matrix, axis=-1, keepdims=True))
    raised = jnp.exp(score_matrix - row_max)
    weights = raised / lax.optimization_barrier(jnp.sum(raised, axis=-1, keepdims=True))
    offset = lax.optimization_barrier(jnp.sum(weights * score_tangent, axis=-1, keepdims=True))
    weights_tan = weights * (score_tangent - offset)
    weight_reduced = reduced_precision(weights)
    tangent_reduced = reduced_precision(weights_tan)
    attention_output = reduced_precision(inner_product('gsf,fgn->sgn', weight_reduced, every_value))
    attention_tangent = reduced_precision(inner_product('gsf,fgn->sgn', tangent_reduced, every_value) + inner_product('gsf,fgn->sgn', weight_reduced, value_tangents))
    weight_gradient = inner_product('zqc,pqc->qzp', output_gradient, every_value) + inner_product('zqc,pqc->qzp', tangent_gradient, value_tangents)
    weight_tangent_gradient = inner_product('zqc,pqc->qzp', tangent_gradient, every_value)
    inner_sum = lax.optimization_barrier(jnp.sum(weights * weight_tangent_gradient, axis=-1, keepdims=True))
    d_scores_tan = weights * (weight_tangent_gradient - inner_sum)
    totals = weight_gradient + weight_tangent_gradient * (score_tangent - offset) - inner_sum * score_tangent
    d_scores = weights * (totals - lax.optimization_barrier(jnp.sum(weights * totals, axis=-1, keepdims=True)))
    score_reduced = reduced_precision(d_scores)
    score_tangent_reduced = reduced_precision(d_scores_tan)
    query_gradient = (scale_factor * (inner_product('gsf,fgn->sgn', score_reduced, every_key) + inner_product('gsf,fgn->sgn', score_tangent_reduced, key_tangents))).astype(jnp.bfloat16)
    query_tangent_gradient = (scale_factor * inner_product('gsf,fgn->sgn', score_tangent_reduced, every_key)).astype(jnp.bfloat16)
    key_gradient = scale_factor * (inner_product('cia,ick->ack', score_reduced, query_block) + inner_product('cia,ick->ack', score_tangent_reduced, query_tangents))
    key_tangent_gradient = scale_factor * inner_product('cia,ick->ack', score_tangent_reduced, query_block)
    value_gradient = inner_product('cia,ick->ack', weight_reduced, output_gradient) + inner_product('cia,ick->ack', tangent_reduced, tangent_gradient)
    value_tangent_gradient = inner_product('cia,ick->ack', weight_reduced, tangent_gradient)
    return ((query_gradient, query_tangent_gradient, attention_output, attention_tangent), (key_gradient, key_tangent_gradient, value_gradient, value_tangent_gradient))

def attention_grads(query_block, query_tangents, output_gradient, tangent_gradient, every_key, key_tangents, every_value, value_tangents):
    count = query_block.shape[0]
    block_rows = min(512, count)
    blocks = count // block_rows
    scale_factor = 1.0 / math.sqrt(query_block.shape[2])

    def advance(running, pieces):
        row_out, col_out = block_terms(pieces[0], pieces[1], pieces[2], pieces[3], every_key, key_tangents, every_value, value_tangents, scale_factor)
        return (tuple((left_sum + right_sum for left_sum, right_sum in zip(running, col_out))), row_out)
    zeros_init = jnp.zeros(every_key.shape, jnp.float32)
    split_rows = tuple((array.reshape((blocks, block_rows) + array.shape[1:]) for array in (query_block, query_tangents, output_gradient, tangent_gradient)))
    running, row_out = lax.scan(advance, (zeros_init, zeros_init, zeros_init, zeros_init), split_rows)
    row_out = tuple((array.reshape((count,) + array.shape[2:]) for array in row_out))
    return (row_out, tuple((array.astype(jnp.bfloat16) for array in running)))

def reference(queries, query_tangent, keys, key_tangent, values, value_tangent, out_gain, grad_y, grad_y_tan):
    gain_full = out_gain.astype(jnp.float32)

    def per_head(array):
        return array.reshape(array.shape[0], HEADS, HEAD_DIM)

    def one_probe(pieces):
        query_rows, query_tangents, key_rows, key_tan, value_rows, value_tan, cot_rows, cot_tan = pieces
        output_gradient = reduced_precision(cot_rows.astype(jnp.float32) * gain_full)
        tangent_gradient = reduced_precision(cot_tan.astype(jnp.float32) * gain_full)
        row_out, col_out = attention_grads(per_head(query_rows), per_head(query_tangents), per_head(output_gradient), per_head(tangent_gradient), per_head(key_rows), per_head(key_tan), per_head(value_rows), per_head(value_tan))
        flat = tuple((array.reshape(array.shape[0], WIDTH) for array in row_out + col_out))
        gain_part = lax.optimization_barrier(jnp.sum(cot_rows.astype(jnp.float32) * flat[2].astype(jnp.float32) + cot_tan.astype(jnp.float32) * flat[3].astype(jnp.float32), axis=0))
        return (flat[0], flat[1], flat[4], flat[5], flat[6], flat[7], gain_part)
    results = lax.map(one_probe, (queries, query_tangent, keys, key_tangent, values, value_tangent, grad_y, grad_y_tan))
    return (results[0], results[1], results[2], results[3], results[4], results[5], lax.optimization_barrier(jnp.sum(results[6], axis=0)))
```

```python
import functools
import math

import jax
import jax.numpy as jnp
from jax import lax
from jax.experimental import pallas as pl
from jax.experimental.pallas import tpu as pltpu
from jax.sharding import PartitionSpec as P

HEAD_DIM = 128
F32 = jnp.float32
BF16 = jnp.bfloat16


def chunk_sizes(heads):
    if heads < 8 or heads % 4:
        return (heads,)
    edge = heads // 8
    return (edge,) + (heads // 4,) * 3 + (edge,)


def dot(left, right, left_dim, right_dim):
    return lax.dot_general(
        left, right, (((left_dim,), (right_dim,)), ((), ())), preferred_element_type=F32
    )


def pack_kernel(where_ref, a_ref, b_ref, c_ref, d_ref, out_ref):
    heads = out_ref.shape[0]
    for h in range(heads):
        for i, ref in enumerate((a_ref, b_ref, c_ref, d_ref)):
            out_ref[h, :, i * HEAD_DIM : (i + 1) * HEAD_DIM] = ref[
                :, h * HEAD_DIM : (h + 1) * HEAD_DIM
            ]


def pack(where, arrays, halves, core_heads, first, count, block, partner_first):
    rows = arrays[0].shape[0]
    steps = count // block

    def column(i, where_ref):
        half = lax.rem(i // steps + where_ref[0] + (1 if partner_first else 0), 2)
        return (0, (half * core_heads + first) // block + lax.rem(i, steps))

    return pl.pallas_call(
        pack_kernel,
        grid_spec=pltpu.PrefetchScalarGridSpec(
            num_scalar_prefetch=1,
            grid=(halves * steps,),
            in_specs=[pl.BlockSpec((rows, block * HEAD_DIM), column)] * 4,
            out_specs=pl.BlockSpec(
                (block, rows, 4 * HEAD_DIM), lambda i, where_ref: (i, 0, 0)
            ),
        ),
        out_shape=jax.ShapeDtypeStruct((halves * count, rows, 4 * HEAD_DIM), BF16),
        cost_estimate=pl.CostEstimate(
            flops=0, bytes_accessed=halves * count * rows * 4 * HEAD_DIM * 4, transcendentals=0
        ),
    )(where, *arrays)


def attention_kernel(chips, scale, where_ref, *refs):
    q_ref, qt_ref, gy_ref, gyt_ref, gain_ref, qs_ref, own_ref = refs[:7]
    a_refs = refs[7 : 6 + chips]
    b_ref = refs[6 + chips]
    dq_ref, dqs_ref, da_ref, db_ref, d0_ref, gain_out, kbuf, dbuf = refs[7 + chips :]
    reach = where_ref[1]
    half_rows = own_ref.shape[3]
    rows_k = 2 * half_rows
    d = HEAD_DIM

    kbuf[0] = own_ref[...].reshape(rows_k, 4 * d)
    for j in range(1, chips):

        @pl.when(reach >= j)
        def _(j=j):
            kbuf[j] = a_refs[j - 1][...].reshape(rows_k, 4 * d)

        @pl.when(reach < j)
        def _(j=j):
            kbuf[j] = b_ref[jnp.clip(j - reach - 1, 0, chips - 2)].reshape(rows_k, 4 * d)

    every = kbuf[...].reshape(chips * rows_k, 4 * d)
    k, k_kt = every[:, :d], every[:, : 2 * d]
    v, v_vt = every[:, 2 * d : 3 * d], every[:, 2 * d :]
    swapped = qs_ref[0]
    q = jnp.concatenate([q_ref[...], swapped[:, :d]], axis=0)
    qt = jnp.concatenate([qt_ref[...], swapped[:, d : 2 * d]], axis=0)
    gy = jnp.concatenate([gy_ref[...], swapped[:, 2 * d : 3 * d]], axis=0).astype(F32)
    gyt = jnp.concatenate([gyt_ref[...], swapped[:, 3 * d :]], axis=0).astype(F32)
    gain = gain_ref[...].astype(F32)
    go = (gy * gain).astype(BF16)
    got = (gyt * gain).astype(BF16)

    scores = dot(q, k, 1, 1) * scale
    scores_tan = dot(jnp.concatenate([qt, q], axis=1), k_kt, 1, 1) * scale
    top = jnp.max(scores, axis=-1, keepdims=True)
    raised = jnp.exp(scores - top)
    probs = raised * (1.0 / jnp.sum(raised, axis=-1, keepdims=True))
    offset = jnp.sum(probs * scores_tan, axis=-1, keepdims=True)
    centred = scores_tan - offset
    probs_tan = probs * centred
    p_low = probs.astype(BF16)
    pt_low = probs_tan.astype(BF16)
    go_got = jnp.concatenate([go, got], axis=1)
    d_probs = dot(go_got, v_vt, 1, 1)
    d_probs_tan = dot(got, v, 1, 1)
    inner = jnp.sum(probs * d_probs_tan, axis=-1, keepdims=True)
    dst = probs * (d_probs_tan - inner)
    totals = d_probs + d_probs_tan * centred - inner * scores_tan
    ds = probs * (totals - jnp.sum(probs * totals, axis=-1, keepdims=True))
    ds_low = ds.astype(BF16)
    dst_low = dst.astype(BF16)

    out_pair = dot(p_low, v_vt, 1, 0)
    attn_out = out_pair[:, :d].astype(BF16).astype(F32)
    attn_tan = (dot(pt_low, v, 1, 0) + out_pair[:, d:]).astype(BF16).astype(F32)
    gain_out[0] = jnp.sum(gy * attn_out + gyt * attn_tan, axis=0, keepdims=True)

    q_pair = dot(dst_low, k_kt, 1, 0)
    dq = (scale * (dot(ds_low, k, 1, 0) + q_pair[:, d:])).astype(BF16)
    dqt = (scale * q_pair[:, :d]).astype(BF16)
    rows_q = q_ref.shape[0]
    dq_ref[0] = dq[:rows_q]
    dq_ref[1] = dqt[:rows_q]
    dqs_ref[0] = dq[rows_q:]
    dqs_ref[1] = dqt[rows_q:]

    k_pair = dot(dst_low, jnp.concatenate([q, qt], axis=1), 0, 0)
    dk = scale * (dot(ds_low, q, 0, 0) + k_pair[:, d:])
    dkt = scale * k_pair[:, :d]
    v_pair = dot(p_low, go_got, 0, 0)
    dv = v_pair[:, :d] + dot(pt_low, got, 0, 0)
    dvt = v_pair[:, d:]
    for i, part in enumerate((dk, dkt, dv, dvt)):
        columns = slice(i * d, (i + 1) * d)
        d0_ref[:, 0, :, columns] = part[:rows_k].reshape(2, half_rows, d)
        dbuf[:, :, columns] = part.astype(BF16).reshape(chips, rows_k, d)
    for j in range(1, chips):
        da_ref[j - 1] = dbuf[j].reshape(2, 1, half_rows, 4 * d)
        db_ref[j - 1] = dbuf[jnp.minimum(reach + j, chips - 1)].reshape(2, 1, half_rows, 4 * d)


def attention(where, rows_in, gain, swapped, own, along, other, core_heads, first):
    chips = len(along) + 1
    rows_q = rows_in[0].shape[0]
    heads, half_rows = own.shape[2], own.shape[3]
    rows_k = 2 * half_rows
    d = HEAD_DIM

    def column(h, where_ref):
        return (0, where_ref[0] * core_heads + first + h)

    payload = pl.BlockSpec((1, 2, 1, half_rows, 4 * d), lambda h, where_ref: (0, 0, h, 0, 0))
    slots = pl.BlockSpec(
        (chips - 1, 2, 1, half_rows, 4 * d), lambda h, where_ref: (0, 0, h, 0, 0)
    )
    queries_out = pl.BlockSpec((2, rows_q, d), lambda h, where_ref: (0, 0, h))
    pairs = heads * 2 * rows_q * chips * rows_k
    return pl.pallas_call(
        functools.partial(attention_kernel, chips, 1.0 / math.sqrt(d)),
        grid_spec=pltpu.PrefetchScalarGridSpec(
            num_scalar_prefetch=1,
            grid=(heads,),
            in_specs=[pl.BlockSpec((rows_q, d), column)] * 4
            + [
                pl.BlockSpec((1, d), column),
                pl.BlockSpec((1, rows_q, 4 * d), lambda h, where_ref: (first + h, 0, 0)),
            ]
            + [payload] * chips
            + [slots],
            out_specs=[
                queries_out,
                queries_out,
                slots,
                slots,
                pl.BlockSpec((2, 1, half_rows, 4 * d), lambda h, where_ref: (0, h, 0, 0)),
                pl.BlockSpec((1, 1, d), lambda h, where_ref: (h, 0, 0)),
            ],
            scratch_shapes=[
                pltpu.VMEM((chips, rows_k, 4 * d), BF16),
                pltpu.VMEM((chips, rows_k, 4 * d), BF16),
            ],
        ),
        out_shape=[
            jax.ShapeDtypeStruct((2, rows_q, heads * d), BF16),
            jax.ShapeDtypeStruct((2, rows_q, heads * d), BF16),
            jax.ShapeDtypeStruct((chips - 1, 2, heads, half_rows, 4 * d), BF16),
            jax.ShapeDtypeStruct((chips - 1, 2, heads, half_rows, 4 * d), BF16),
            jax.ShapeDtypeStruct((2, heads, half_rows, 4 * d), F32),
            jax.ShapeDtypeStruct((heads, 1, d), F32),
        ],
        compiler_params=pltpu.CompilerParams(vmem_limit_bytes=48 * 1024 * 1024),
        cost_estimate=pl.CostEstimate(
            flops=pairs * 36 * d, bytes_accessed=pairs * 16, transcendentals=pairs
        ),
    )(where, *rows_in, gain, swapped, own, *along, other)


def finish_kernel(where_ref, kept_ref, came_ref, *refs):
    total = kept_ref[...].astype(F32) + came_ref[...].astype(F32)
    heads = kept_ref.shape[1]
    for i, ref in enumerate(refs[-4:]):
        for h in range(heads):
            ref[:, h * HEAD_DIM : (h + 1) * HEAD_DIM] = total[
                0, h, :, i * HEAD_DIM : (i + 1) * HEAD_DIM
            ].astype(BF16)


def finish(where, kept, came, before, width, core_heads, first):
    heads, rows = kept.shape[1], kept.shape[2]
    block = math.gcd(heads, first) if first else heads
    steps = heads // block

    def column(i, where_ref):
        half = lax.rem(i // steps + where_ref[0], 2)
        return (0, (half * core_heads + first) // block + lax.rem(i, steps))

    old = list(before or ())
    return pl.pallas_call(
        finish_kernel,
        grid_spec=pltpu.PrefetchScalarGridSpec(
            num_scalar_prefetch=1,
            grid=(2 * steps,),
            in_specs=[
                pl.BlockSpec(
                    (1, block, rows, 4 * HEAD_DIM),
                    lambda i, where_ref: (i // steps, lax.rem(i, steps), 0, 0),
                ),
                pl.BlockSpec(
                    (1, block, rows, 4 * HEAD_DIM),
                    lambda i, where_ref: (1 - i // steps, lax.rem(i, steps), 0, 0),
                ),
            ]
            + [pl.BlockSpec(memory_space=pl.ANY)] * len(old),
            out_specs=[pl.BlockSpec((rows, block * HEAD_DIM), column)] * 4,
        ),
        out_shape=[jax.ShapeDtypeStruct((rows, width), BF16)] * 4,
        input_output_aliases={3 + i: i for i in range(len(old))},
        cost_estimate=pl.CostEstimate(
            flops=0, bytes_accessed=heads * rows * HEAD_DIM * 48, transcendentals=0
        ),
    )(where, kept, came, *old)


def per_device(
    queries, query_tangent, keys, key_tangent, values, value_tangent, out_gain, grad_y, grad_y_tan
):
    count = lax.axis_size("ctx")
    chips = count // 2
    width = queries.shape[2]
    core_heads = width // HEAD_DIM // 2
    place = lax.axis_index("ctx")
    core, chip = lax.rem(place, 2), place // 2
    where = jnp.stack([core, jnp.where(core == 0, chip, chips - 1 - chip)]).astype(jnp.int32)

    swap_pairs = [(i, i ^ 1) for i in range(count)]

    def swap(array):
        return lax.ppermute(array, "ctx", swap_pairs)

    def outward(array, step):
        pairs = [(2 * z, 2 * z + 2) for z in range(step - 1, chips - 1)]
        pairs += [(2 * z + 1, 2 * z - 1) for z in range(1, chips - step + 1)]
        return lax.ppermute(array, "ctx", pairs)

    def homeward(array, far):
        pairs = [(2 * z, 2 * z - 2) for z in range(far, chips)]
        pairs += [(2 * z + 1, 2 * z + 3) for z in range(0, chips - far)]
        return lax.ppermute(array, "ctx", pairs)

    rows_in = (queries[0], query_tangent[0], grad_y[0], grad_y_tan[0])
    key_in = (keys[0], key_tangent[0], values[0], value_tangent[0])
    rows_k = key_in[0].shape[0]
    gain = out_gain.reshape(1, width)
    sizes = chunk_sizes(core_heads)
    starts = [sum(sizes[:i]) for i in range(len(sizes))]

    owns = []
    for first, heads in zip(starts, sizes):
        block = math.gcd(heads, first) if first else heads
        mine = pack(where, key_in, 2, core_heads, first, heads, block, False)
        mine = mine.reshape(2, heads, rows_k, 4 * HEAD_DIM)
        theirs = swap(mine)
        owns.append(jnp.stack([mine, theirs[::-1]], axis=1))

    packed_rows = pack(
        where, rows_in, 1, core_heads, 0, core_heads, math.gcd(core_heads, 4), True
    )
    swapped = swap(packed_rows)

    gradients = None
    parts, sent, gains = [], [], []
    for index, (first, heads) in enumerate(zip(starts, sizes)):
        along = []
        moving = owns[index]
        for step in range(1, chips):
            moving = outward(moving, step)
            along.append(moving)
        other = swap(jnp.stack([a[1] for a in along]))
        dq, dq_other, d_along, d_other, d_own, gain_part = attention(
            where, rows_in, gain, swapped, owns[index], along, other, core_heads, first
        )
        gains.append(gain_part.reshape(heads * HEAD_DIM))
        parts.append(dq)
        sent.append(dq_other)
        d_theirs = swap(d_other)
        arrived = None
        for far in range(chips - 1, 0, -1):
            payload = jnp.stack([d_along[far - 1], d_theirs[far - 1]])
            if arrived is not None:
                payload = (payload.astype(F32) + arrived.astype(F32)).astype(BF16)
            arrived = homeward(payload, far)
        total = arrived.astype(F32)
        total = jnp.stack([total[0] + d_own, total[1]]).astype(BF16)
        came = swap(total[:, 1])
        gradients = finish(
            where, total[:, 0], came, gradients, width, core_heads, first
        )

    dq_mine = jnp.concatenate(parts, axis=2)
    dq_theirs = swap(jnp.concatenate(sent, axis=2))
    halves = jnp.where(
        core == 0,
        jnp.concatenate([dq_mine, dq_theirs], axis=2),
        jnp.concatenate([dq_theirs, dq_mine], axis=2),
    )
    gain_mine = jnp.concatenate(gains)
    gain_zero = jnp.zeros_like(gain_mine)
    gain_all = jnp.where(
        core == 0,
        jnp.concatenate([gain_mine, gain_zero]),
        jnp.concatenate([gain_zero, gain_mine]),
    )
    gain_all = lax.psum(gain_all, ("dp", "ctx"))
    gain_grad = lax.dynamic_slice_in_dim(gain_all, place * (width // count), width // count)
    return (halves[0][None], halves[1][None]) + tuple(g[None] for g in gradients) + (gain_grad,)


def solution(mesh):
    tokens = P("dp", "ctx", None)
    return jax.shard_map(
        per_device,
        mesh=mesh,
        in_specs=(tokens,) * 6 + (P(),) + (tokens,) * 2,
        out_specs=(tokens,) * 6 + (P("ctx"),),
        check_vma=False,
    )
```

```python
import functools
import math

import jax
import jax.numpy as jnp
from jax import lax
from jax.experimental import pallas as pl
from jax.experimental.pallas import tpu as pltpu
from jax.sharding import PartitionSpec as P

HEAD_DIM = 128
F32 = jnp.float32
BF16 = jnp.bfloat16


def chunk_sizes(heads):
    if heads < 8 or heads % 4:
        return (heads,)
    edge = heads // 8
    return (edge,) + (heads // 4,) * 3 + (edge,)


def dot(left, right, left_dim, right_dim):
    return lax.dot_general(
        left, right, (((left_dim,), (right_dim,)), ((), ())), preferred_element_type=F32
    )


def pack_kernel(where_ref, a_ref, b_ref, c_ref, d_ref, out_ref):
    heads = out_ref.shape[0]
    for h in range(heads):
        for i, ref in enumerate((a_ref, b_ref, c_ref, d_ref)):
            out_ref[h, :, i * HEAD_DIM : (i + 1) * HEAD_DIM] = ref[
                :, h * HEAD_DIM : (h + 1) * HEAD_DIM
            ]


def pack(where, arrays, halves, core_heads, first, count, block, partner_first):
    rows = arrays[0].shape[0]
    steps = count // block

    def column(i, where_ref):
        half = lax.rem(i // steps + where_ref[0] + (1 if partner_first else 0), 2)
        return (0, (half * core_heads + first) // block + lax.rem(i, steps))

    return pl.pallas_call(
        pack_kernel,
        grid_spec=pltpu.PrefetchScalarGridSpec(
            num_scalar_prefetch=1,
            grid=(halves * steps,),
            in_specs=[pl.BlockSpec((rows, block * HEAD_DIM), column)] * 4,
            out_specs=pl.BlockSpec(
                (block, rows, 4 * HEAD_DIM), lambda i, where_ref: (i, 0, 0)
            ),
        ),
        out_shape=jax.ShapeDtypeStruct((halves * count, rows, 4 * HEAD_DIM), BF16),
        cost_estimate=pl.CostEstimate(
            flops=0, bytes_accessed=halves * count * rows * 4 * HEAD_DIM * 4, transcendentals=0
        ),
    )(where, *arrays)


def attention_kernel(chips, extra, scale, where_ref, *refs):
    q_ref, qt_ref, gy_ref, gyt_ref, gain_ref, qs_ref, own_ref = refs[:7]
    a_refs = refs[7 : 6 + chips]
    b_ref = refs[6 + chips]
    outs = refs[7 + chips + extra :]
    dq_ref, dqs_ref, db_ref, d0_ref, gain_out = outs[:5]
    da_refs = outs[5 : 4 + chips]
    kbuf, dbuf = outs[4 + chips :]
    reach = where_ref[1]
    half_rows = own_ref.shape[3]
    rows_k = 2 * half_rows
    d = HEAD_DIM

    kbuf[0] = own_ref[...].reshape(rows_k, 4 * d)
    for j in range(1, chips):

        @pl.when(reach >= j)
        def _(j=j):
            kbuf[j] = a_refs[j - 1][...].reshape(rows_k, 4 * d)

        @pl.when(reach < j)
        def _(j=j):
            kbuf[j] = b_ref[jnp.clip(j - reach - 1, 0, chips - 2)].reshape(rows_k, 4 * d)

    every = kbuf[...].reshape(chips * rows_k, 4 * d)
    k, k_kt = every[:, :d], every[:, : 2 * d]
    v, v_vt = every[:, 2 * d : 3 * d], every[:, 2 * d :]
    swapped = qs_ref[0]
    q = jnp.concatenate([q_ref[...], swapped[:, :d]], axis=0)
    qt = jnp.concatenate([qt_ref[...], swapped[:, d : 2 * d]], axis=0)
    gy = jnp.concatenate([gy_ref[...], swapped[:, 2 * d : 3 * d]], axis=0).astype(F32)
    gyt = jnp.concatenate([gyt_ref[...], swapped[:, 3 * d :]], axis=0).astype(F32)
    gain = gain_ref[...].astype(F32)
    go = (gy * gain).astype(BF16)
    got = (gyt * gain).astype(BF16)

    scores = dot(q, k, 1, 1) * scale
    scores_tan = dot(jnp.concatenate([qt, q], axis=1), k_kt, 1, 1) * scale
    top = jnp.max(scores, axis=-1, keepdims=True)
    raised = jnp.exp(scores - top)
    probs = raised * (1.0 / jnp.sum(raised, axis=-1, keepdims=True))
    offset = jnp.sum(probs * scores_tan, axis=-1, keepdims=True)
    centred = scores_tan - offset
    probs_tan = probs * centred
    p_low = probs.astype(BF16)
    pt_low = probs_tan.astype(BF16)
    go_got = jnp.concatenate([go, got], axis=1)
    d_probs = dot(go_got, v_vt, 1, 1)
    d_probs_tan = dot(got, v, 1, 1)
    inner = jnp.sum(probs * d_probs_tan, axis=-1, keepdims=True)
    dst = probs * (d_probs_tan - inner)
    totals = d_probs + d_probs_tan * centred - inner * scores_tan
    ds = probs * (totals - jnp.sum(probs * totals, axis=-1, keepdims=True))
    ds_low = ds.astype(BF16)
    dst_low = dst.astype(BF16)

    out_pair = dot(p_low, v_vt, 1, 0)
    attn_out = out_pair[:, :d].astype(BF16).astype(F32)
    attn_tan = (dot(pt_low, v, 1, 0) + out_pair[:, d:]).astype(BF16).astype(F32)
    gain_out[0] = jnp.sum(gy * attn_out + gyt * attn_tan, axis=0, keepdims=True)

    q_pair = dot(dst_low, k_kt, 1, 0)
    dq = (scale * (dot(ds_low, k, 1, 0) + q_pair[:, d:])).astype(BF16)
    dqt = (scale * q_pair[:, :d]).astype(BF16)
    rows_q = q_ref.shape[0]
    dq_ref[0] = dq[:rows_q]
    dq_ref[1] = dqt[:rows_q]
    dqs_ref[0] = dq[rows_q:]
    dqs_ref[1] = dqt[rows_q:]

    k_pair = dot(dst_low, jnp.concatenate([q, qt], axis=1), 0, 0)
    dk = scale * (dot(ds_low, q, 0, 0) + k_pair[:, d:])
    dkt = scale * k_pair[:, :d]
    v_pair = dot(p_low, go_got, 0, 0)
    dv = v_pair[:, :d] + dot(pt_low, got, 0, 0)
    dvt = v_pair[:, d:]
    for i, part in enumerate((dk, dkt, dv, dvt)):
        columns = slice(i * d, (i + 1) * d)
        d0_ref[:, 0, :, columns] = part[:rows_k].reshape(2, half_rows, d)
        dbuf[:, :, columns] = part.astype(BF16).reshape(chips, rows_k, d)
    for j in range(1, chips):
        da_refs[j - 1][...] = dbuf[j].reshape(2, 1, half_rows, 4 * d)
        db_ref[j - 1] = dbuf[jnp.minimum(reach + j, chips - 1)].reshape(2, 1, half_rows, 4 * d)


def attention(where, rows_in, gain, swapped, own, along, other, core_heads, first, before):
    chips = len(along) + 1
    rows_q = rows_in[0].shape[0]
    heads, half_rows = own.shape[2], own.shape[3]
    rows_k = 2 * half_rows
    d = HEAD_DIM

    def column(h, where_ref):
        return (0, where_ref[0] * core_heads + first + h)

    payload = pl.BlockSpec((1, 2, 1, half_rows, 4 * d), lambda h, where_ref: (0, 0, h, 0, 0))
    slots = pl.BlockSpec(
        (chips - 1, 2, 1, half_rows, 4 * d), lambda h, where_ref: (0, 0, h, 0, 0)
    )
    queries_out = pl.BlockSpec((2, rows_q, d), lambda h, where_ref: (0, 0, h))
    pairs = heads * 2 * rows_q * chips * rows_k
    return pl.pallas_call(
        functools.partial(attention_kernel, chips, len(before), 1.0 / math.sqrt(d)),
        grid_spec=pltpu.PrefetchScalarGridSpec(
            num_scalar_prefetch=1,
            grid=(heads,),
            in_specs=[pl.BlockSpec((rows_q, d), column)] * 4
            + [
                pl.BlockSpec((1, d), column),
                pl.BlockSpec((1, rows_q, 4 * d), lambda h, where_ref: (first + h, 0, 0)),
            ]
            + [payload] * chips
            + [slots]
            + [pl.BlockSpec(memory_space=pl.ANY)] * len(before),
            out_specs=[
                queries_out,
                queries_out,
                slots,
                pl.BlockSpec((2, 1, half_rows, 4 * d), lambda h, where_ref: (0, h, 0, 0)),
                pl.BlockSpec((1, 1, d), lambda h, where_ref: (h, 0, 0)),
            ]
            + [pl.BlockSpec((2, 1, half_rows, 4 * d), lambda h, where_ref: (0, h, 0, 0))]
            * (chips - 1),
            scratch_shapes=[
                pltpu.VMEM((chips, rows_k, 4 * d), BF16),
                pltpu.VMEM((chips, rows_k, 4 * d), BF16),
            ],
        ),
        out_shape=[
            jax.ShapeDtypeStruct((2, rows_q, heads * d), BF16),
            jax.ShapeDtypeStruct((2, rows_q, heads * d), BF16),
            jax.ShapeDtypeStruct((chips - 1, 2, heads, half_rows, 4 * d), BF16),
            jax.ShapeDtypeStruct((2, heads, half_rows, 4 * d), F32),
            jax.ShapeDtypeStruct((heads, 1, d), F32),
        ]
        + [jax.ShapeDtypeStruct((2, heads, half_rows, 4 * d), BF16)] * (chips - 1),
        compiler_params=pltpu.CompilerParams(vmem_limit_bytes=48 * 1024 * 1024),
        cost_estimate=pl.CostEstimate(
            flops=pairs * 36 * d, bytes_accessed=pairs * 16, transcendentals=pairs
        ),
    )(where, *rows_in, gain, swapped, own, *along, other, *before)


def finish_kernel(where_ref, arrived_ref, own_ref, came_ref, *refs):
    half = pl.program_id(0) // (pl.num_programs(0) // 2)
    heads = came_ref.shape[1]
    mine = jnp.where(half == 0, own_ref[0], jnp.zeros_like(own_ref[0]))
    total = arrived_ref[0, 0].astype(F32) + came_ref[0].astype(F32) + mine
    for i, ref in enumerate(refs[-4:]):
        for h in range(heads):
            ref[:, h * HEAD_DIM : (h + 1) * HEAD_DIM] = total[
                h, :, i * HEAD_DIM : (i + 1) * HEAD_DIM
            ].astype(BF16)


def finish(where, arrived, own, came, before, width, core_heads, first):
    heads, rows = came.shape[1], came.shape[2]
    block = math.gcd(heads, first) if first else heads
    steps = heads // block

    def column(i, where_ref):
        half = lax.rem(i // steps + where_ref[0], 2)
        return (0, (half * core_heads + first) // block + lax.rem(i, steps))

    old = list(before or ())
    size = (block, rows, 4 * HEAD_DIM)
    return pl.pallas_call(
        finish_kernel,
        grid_spec=pltpu.PrefetchScalarGridSpec(
            num_scalar_prefetch=1,
            grid=(2 * steps,),
            in_specs=[
                pl.BlockSpec(
                    (1, 1) + size, lambda i, where_ref: (i // steps, 0, lax.rem(i, steps), 0, 0)
                ),
                pl.BlockSpec((1,) + size, lambda i, where_ref: (0, lax.rem(i, steps), 0, 0)),
                pl.BlockSpec(
                    (1,) + size, lambda i, where_ref: (1 - i // steps, lax.rem(i, steps), 0, 0)
                ),
            ]
            + [pl.BlockSpec(memory_space=pl.ANY)] * len(old),
            out_specs=[pl.BlockSpec((rows, block * HEAD_DIM), column)] * 4,
        ),
        out_shape=[jax.ShapeDtypeStruct((rows, width), BF16)] * 4,
        input_output_aliases={4 + i: i for i in range(len(old))},
        cost_estimate=pl.CostEstimate(
            flops=0, bytes_accessed=heads * rows * HEAD_DIM * 48, transcendentals=0
        ),
    )(where, arrived, own, came, *old)


def after(array, *before):
    return lax.optimization_barrier((array,) + before)[0] if before else array


def sum_over(array, axis):
    size = lax.axis_size(axis)
    if size & (size - 1):
        return lax.psum(array, axis)
    far = 1
    while far < size:
        array = array + lax.ppermute(array, axis, [(i, i ^ far) for i in range(size)])
        far *= 2
    return array


def per_device(
    queries, query_tangent, keys, key_tangent, values, value_tangent, out_gain, grad_y, grad_y_tan
):
    count = lax.axis_size("ctx")
    chips = count // 2
    width = queries.shape[2]
    core_heads = width // HEAD_DIM // 2
    place = lax.axis_index("ctx")
    core, chip = lax.rem(place, 2), place // 2
    where = jnp.stack([core, jnp.where(core == 0, chip, chips - 1 - chip)]).astype(jnp.int32)

    swap_pairs = [(i, i ^ 1) for i in range(count)]

    def swap(array):
        return lax.ppermute(array, "ctx", swap_pairs)

    def outward(array, step):
        pairs = [(2 * z, 2 * z + 2) for z in range(step - 1, chips - 1)]
        pairs += [(2 * z + 1, 2 * z - 1) for z in range(1, chips - step + 1)]
        return lax.ppermute(array, "ctx", pairs)

    def homeward(array, far):
        pairs = [(2 * z, 2 * z - 2) for z in range(far, chips)]
        pairs += [(2 * z + 1, 2 * z + 3) for z in range(0, chips - far)]
        return lax.ppermute(array, "ctx", pairs)

    rows_in = (queries[0], query_tangent[0], grad_y[0], grad_y_tan[0])
    key_in = (keys[0], key_tangent[0], values[0], value_tangent[0])
    rows_k = key_in[0].shape[0]
    gain = out_gain.reshape(1, width)
    sizes = chunk_sizes(core_heads)
    starts = [sum(sizes[:i]) for i in range(len(sizes))]

    owns = []
    for first, heads in zip(starts, sizes):
        block = math.gcd(heads, first) if first else heads
        mine = pack(where, key_in, 2, core_heads, first, heads, block, False)
        mine = mine.reshape(2, heads, rows_k, 4 * HEAD_DIM)
        theirs = swap(mine)
        owns.append(jnp.stack([mine, theirs[::-1]], axis=1))

    packed_rows = pack(
        where, rows_in, 1, core_heads, 0, core_heads, math.gcd(core_heads, 4), True
    )
    swapped = swap(packed_rows)

    parts = len(sizes)
    along = [[] for _ in sizes]
    results = [None] * parts
    arrived = [None] * parts
    gradients = None

    def gather(index, *before):
        step = len(along[index]) + 1
        moving = along[index][-1] if along[index] else owns[index]
        along[index].append(outward(after(moving, *before), step))

    def attend(index, *before):
        first = starts[index]
        other = swap(jnp.stack([a[1] for a in along[index]]))
        out = attention(
            where,
            rows_in,
            gain,
            swapped,
            owns[index],
            along[index],
            other,
            core_heads,
            first,
            before,
        )
        results[index] = (out[0], out[1], out[3], out[4], out[5:], swap(out[2]))
        return out[3]

    def homewards(index, far, *before):
        d_along, d_theirs = results[index][4:]
        payload = jnp.stack([d_along[far - 1], d_theirs[far - 1]])
        if arrived[index] is not None:
            payload = (payload.astype(F32) + arrived[index].astype(F32)).astype(BF16)
        arrived[index] = homeward(after(payload, *before), far)

    def conclude(index, gradients):
        own = results[index][2]
        leaving = jnp.stack(
            [arrived[index][0, 1].astype(F32) + own[1], arrived[index][1, 1].astype(F32)]
        ).astype(BF16)
        return finish(
            where,
            arrived[index],
            own,
            swap(leaving),
            gradients,
            width,
            core_heads,
            starts[index],
        )

    for step in range(1, chips):
        gather(0)
    gather(1, along[0][0])
    if parts > 2:
        gather(2, along[0][1])
    ready = along[0][-1]
    for index in range(parts):
        if index + 1 < parts:
            while len(along[index + 1]) < chips - 2:
                gather(index + 1, ready)
        if index:
            homewards(index - 1, chips - 2, ready)
        done = attend(index)
        if index + 1 < parts:
            gather(index + 1, done)
        if index + 3 < parts:
            gather(index + 3, done)
        if index:
            for far in range(chips - 3, 0, -1):
                homewards(index - 1, far, done)
        homewards(index, chips - 1)
        if index + 1 < parts:
            ready = along[index + 1][-1]
        if index > 1:
            gradients = conclude(index - 2, gradients)
    gain_mine = jnp.concatenate([r[3].reshape(-1) for r in results])
    gain_zero = jnp.zeros_like(gain_mine)
    gain_all = jnp.where(
        core == 0,
        jnp.concatenate([gain_mine, gain_zero]),
        jnp.concatenate([gain_zero, gain_mine]),
    ).reshape(count, width // count)
    gain_all = lax.all_to_all(gain_all, "ctx", split_axis=0, concat_axis=0, tiled=True)
    gain_grad = sum_over(jnp.sum(gain_all, axis=0), "dp")
    for far in range(chips - 2, 0, -1):
        homewards(parts - 1, far)
    gradients = conclude(parts - 2, gradients)
    gradients = conclude(parts - 1, gradients)

    dq_mine = jnp.concatenate([r[0] for r in results], axis=2)
    dq_theirs = swap(jnp.concatenate([r[1] for r in results], axis=2))
    halves = jnp.where(
        core == 0,
        jnp.concatenate([dq_mine, dq_theirs], axis=2),
        jnp.concatenate([dq_theirs, dq_mine], axis=2),
    )
    return (halves[0][None], halves[1][None]) + tuple(g[None] for g in gradients) + (gain_grad,)


def solution(mesh):
    tokens = P("dp", "ctx", None)
    return jax.shard_map(
        per_device,
        mesh=mesh,
        in_specs=(tokens,) * 6 + (P(),) + (tokens,) * 2,
        out_specs=(tokens,) * 6 + (P("ctx"),),
        check_vma=False,
    )
```

```python
import functools
import math

import jax
import jax.numpy as jnp
from jax import lax
from jax.experimental import pallas as pl
from jax.experimental.pallas import tpu as pltpu
from jax.sharding import PartitionSpec as P

HEAD_DIM = 128
MEMBERS = 4
F32 = jnp.float32
BF16 = jnp.bfloat16


def dot(left, right, left_dim, right_dim):
    return lax.dot_general(
        left, right, (((left_dim,), (right_dim,)), ((), ())), preferred_element_type=F32
    )


def pack_kernel(a_ref, b_ref, c_ref, d_ref, out_ref):
    for h in range(out_ref.shape[1]):
        for i, ref in enumerate((a_ref, b_ref, c_ref, d_ref)):
            out_ref[0, h, :, i * HEAD_DIM : (i + 1) * HEAD_DIM] = ref[
                :, h * HEAD_DIM : (h + 1) * HEAD_DIM
            ]


def pack(arrays, local_heads, first, count, block):
    rows = arrays[0].shape[0]
    steps = count // block

    def column(member, i):
        return (0, (member * local_heads + first) // block + i)

    return pl.pallas_call(
        pack_kernel,
        grid=(MEMBERS, steps),
        in_specs=[pl.BlockSpec((rows, block * HEAD_DIM), column)] * 4,
        out_specs=pl.BlockSpec(
            (1, block, rows, 4 * HEAD_DIM), lambda member, i: (member, i, 0, 0)
        ),
        out_shape=jax.ShapeDtypeStruct((MEMBERS, count, rows, 4 * HEAD_DIM), BF16),
        cost_estimate=pl.CostEstimate(
            flops=0, bytes_accessed=MEMBERS * count * rows * HEAD_DIM * 16, transcendentals=0
        ),
    )(*arrays)


def unpack_kernel(in_ref, *refs):
    outs = refs[-(in_ref.shape[3] // HEAD_DIM) :]
    for h in range(in_ref.shape[1]):
        for i, ref in enumerate(outs):
            ref[:, h * HEAD_DIM : (h + 1) * HEAD_DIM] = in_ref[
                0, h, :, i * HEAD_DIM : (i + 1) * HEAD_DIM
            ]


def unpack(packed, before, width, local_heads, first):
    count, rows = packed.shape[1], packed.shape[2]
    results = packed.shape[3] // HEAD_DIM
    old = list(before or ())
    return pl.pallas_call(
        unpack_kernel,
        grid=(MEMBERS,),
        in_specs=[
            pl.BlockSpec(
                (1, count, rows, results * HEAD_DIM), lambda member: (member, 0, 0, 0)
            )
        ]
        + [pl.BlockSpec(memory_space=pl.ANY)] * len(old),
        out_specs=[
            pl.BlockSpec(
                (rows, count * HEAD_DIM),
                lambda member: (0, (member * local_heads + first) // count),
            )
        ]
        * results,
        out_shape=[jax.ShapeDtypeStruct((rows, width), BF16)] * results,
        input_output_aliases={1 + i: i for i in range(len(old))},
        cost_estimate=pl.CostEstimate(
            flops=0, bytes_accessed=packed.size * 4, transcendentals=0
        ),
    )(packed, *old)


def attention_kernel(groups, block, scale, rows_ref, gain_ref, *refs):
    key_refs, outs = refs[:groups], refs[groups:]
    dq_ref, gain_out, own_out = outs[:3]
    other_outs = outs[3:]
    d = HEAD_DIM
    members, _, part_rows, _ = rows_ref.shape
    key_rows = key_refs[0].shape[2]
    rows_k = members * key_rows
    every = jnp.concatenate([ref[...].reshape(rows_k, 4 * d) for ref in key_refs], axis=0)
    k, k_kt = every[:, :d], every[:, : 2 * d]
    v, v_vt = every[:, 2 * d : 3 * d], every[:, 2 * d :]
    gain = gain_ref[...].astype(F32)
    sums = None
    step = block // part_rows
    for start in range(0, members, step):
        rows = rows_ref[start : start + step].reshape(block, 4 * d)
        q, qt = rows[:, :d], rows[:, d : 2 * d]
        gy = rows[:, 2 * d : 3 * d].astype(F32)
        gyt = rows[:, 3 * d :].astype(F32)
        go = (gy * gain).astype(BF16)
        got = (gyt * gain).astype(BF16)
        go_got = jnp.concatenate([go, got], axis=1)

        scores = dot(q, k, 1, 1) * scale
        scores_tan = dot(jnp.concatenate([qt, q], axis=1), k_kt, 1, 1) * scale
        d_probs = dot(go_got, v_vt, 1, 1)
        d_probs_tan = dot(got, v, 1, 1)
        top = jnp.max(scores, axis=-1, keepdims=True)
        raised = jnp.exp(scores - top)
        probs = raised * (1.0 / jnp.sum(raised, axis=-1, keepdims=True))
        offset = jnp.sum(probs * scores_tan, axis=-1, keepdims=True)
        centred = scores_tan - offset
        p_low = probs.astype(BF16)
        pt_low = (probs * centred).astype(BF16)
        inner = jnp.sum(probs * d_probs_tan, axis=-1, keepdims=True)
        dst_low = (probs * (d_probs_tan - inner)).astype(BF16)
        totals = d_probs + d_probs_tan * centred - inner * scores_tan
        ds = probs * (totals - jnp.sum(probs * totals, axis=-1, keepdims=True))
        ds_low = ds.astype(BF16)

        out_pair = dot(p_low, v_vt, 1, 0)
        attn_out = out_pair[:, :d].astype(BF16).astype(F32)
        attn_tan = (dot(pt_low, v, 1, 0) + out_pair[:, d:]).astype(BF16).astype(F32)
        gain_sum = jnp.sum(gy * attn_out + gyt * attn_tan, axis=0, keepdims=True)
        q_pair = dot(dst_low, k_kt, 1, 0)
        dq = scale * (dot(ds_low, k, 1, 0) + q_pair[:, d:])
        dqt = scale * q_pair[:, :d]
        both = jnp.concatenate([dq, dqt], axis=1).astype(BF16)
        dq_ref[start : start + step] = both.reshape(step, 1, part_rows, 2 * d)

        k_pair = dot(dst_low, rows[:, : 2 * d], 0, 0)
        v_pair = dot(p_low, go_got, 0, 0)
        terms = (
            dot(ds_low, q, 0, 0) + k_pair[:, d:],
            k_pair[:, :d],
            v_pair[:, :d] + dot(pt_low, got, 0, 0),
            v_pair[:, d:],
            gain_sum,
        )
        sums = terms if sums is None else tuple(a + b for a, b in zip(sums, terms))
    dk, dkt, dv, dvt, gain_sum = sums
    gain_out[0] = gain_sum
    for i, part in enumerate((scale * dk, scale * dkt, dv, dvt)):
        columns = slice(i * d, (i + 1) * d)
        for g, ref in enumerate((own_out,) + other_outs):
            ref[:, 0, :, columns] = (
                part[g * rows_k : (g + 1) * rows_k]
                .reshape(members, key_rows, d)
                .astype(ref.dtype)
            )


def attention(rows, gain, key_parts, gain_column, row_first, heads):
    groups = len(key_parts)
    members, _, part_rows, _ = rows.shape
    key_rows = key_parts[0].shape[2]
    d = HEAD_DIM
    block = 2 * part_rows
    keys_spec = pl.BlockSpec((members, 1, key_rows, 4 * d), lambda h, at: (0, h, 0, 0))
    keys_shape = (members, heads, key_rows, 4 * d)
    pairs = heads * members * part_rows * groups * members * key_rows
    return pl.pallas_call(
        lambda at, *refs: attention_kernel(groups, block, 1.0 / math.sqrt(d), *refs),
        grid_spec=pltpu.PrefetchScalarGridSpec(
            num_scalar_prefetch=1,
            grid=(heads,),
            in_specs=[
                pl.BlockSpec(
                    (members, 1, part_rows, 4 * d), lambda h, at: (0, row_first + h, 0, 0)
                ),
                pl.BlockSpec((1, d), lambda h, at: (0, at[0] + h)),
            ]
            + [keys_spec] * groups,
            out_specs=[
                pl.BlockSpec((members, 1, part_rows, 2 * d), lambda h, at: (0, h, 0, 0)),
                pl.BlockSpec((1, 1, d), lambda h, at: (h, 0, 0)),
            ]
            + [keys_spec] * groups,
        ),
        out_shape=[
            jax.ShapeDtypeStruct((members, heads, part_rows, 2 * d), BF16),
            jax.ShapeDtypeStruct((heads, 1, d), F32),
            jax.ShapeDtypeStruct(keys_shape, F32),
        ]
        + [jax.ShapeDtypeStruct(keys_shape, BF16)] * (groups - 1),
        compiler_params=pltpu.CompilerParams(vmem_limit_bytes=48 * 1024 * 1024),
        cost_estimate=pl.CostEstimate(
            flops=pairs * 36 * d, bytes_accessed=pairs * 8, transcendentals=pairs
        ),
    )(gain_column, rows, gain, *key_parts)


def after(array, *before):
    return lax.optimization_barrier((array,) + before)[0] if before else array


def sum_over(array, axis):
    size = lax.axis_size(axis)
    if size & (size - 1):
        return lax.psum(array, axis)
    far = 1
    while far < size:
        array = array + lax.ppermute(array, axis, [(i, i ^ far) for i in range(size)])
        far *= 2
    return array


def per_device(
    queries, query_tangent, keys, key_tangent, values, value_tangent, out_gain, grad_y, grad_y_tan
):
    count = lax.axis_size("ctx")
    groups = count // MEMBERS
    width = queries.shape[2]
    local_heads = width // HEAD_DIM // MEMBERS
    place = lax.axis_index("ctx")
    member = lax.rem(place, MEMBERS)
    teams = [[g * MEMBERS + i for i in range(MEMBERS)] for g in range(groups)]

    def exchange(array):
        return lax.all_to_all(
            array, "ctx", split_axis=0, concat_axis=0, tiled=True, axis_index_groups=teams
        )

    def shift(array, far):
        pairs = [(i, (i + far * MEMBERS) % count) for i in range(count)]
        return lax.ppermute(array, "ctx", pairs)

    rows_in = (queries[0], query_tangent[0], grad_y[0], grad_y_tan[0])
    key_in = (keys[0], key_tangent[0], values[0], value_tangent[0])
    gain = out_gain.reshape(1, width)
    size = max(1, local_heads // 4)
    parts = local_heads // size

    key_first = exchange(pack(key_in, local_heads, 0, size, size))
    key_rest = exchange(
        after(pack(key_in, local_heads, size, local_heads - size, size), key_first)
    )
    rows_first = exchange(after(pack(rows_in, local_heads, 0, size, size), key_rest))
    rows_rest = exchange(
        after(pack(rows_in, local_heads, size, local_heads - size, size), rows_first)
    )

    owns, others = [], []
    for index in range(parts):
        own = key_first if index == 0 else key_rest[:, (index - 1) * size : index * size]
        owns.append(own)
        others.append([shift(own, far) for far in range(1, groups)])

    results = []
    for index in range(parts):
        column = (member * local_heads + index * size).astype(jnp.int32).reshape(1)
        out = attention(
            rows_first if index == 0 else rows_rest,
            gain,
            [owns[index]] + others[index],
            column,
            0 if index == 0 else (index - 1) * size,
            size,
        )
        total = out[2]
        for far in range(1, groups):
            total = total + shift(out[2 + far], -far).astype(F32)
        results.append((out[0], out[1], total.astype(BF16)))

    def back(which, indices):
        return exchange(jnp.concatenate([results[i][which] for i in indices], axis=1))

    query_grads = key_grads = None
    half = parts // 2
    for indices in (range(half), range(half, parts)):
        query_grads = unpack(
            back(0, indices), query_grads, width, local_heads, indices[0] * size
        )
    gain_mine = jnp.concatenate([r[1] for r in results]).reshape(-1)
    gain_all = lax.dynamic_update_slice_in_dim(
        jnp.zeros((width,), F32), gain_mine, member * (width // MEMBERS), 0
    ).reshape(count, width // count)
    gain_all = lax.all_to_all(gain_all, "ctx", split_axis=0, concat_axis=0, tiled=True)
    gain_grad = sum_over(jnp.sum(gain_all, axis=0), "dp")
    for indices in (range(half),) + tuple(range(i, i + 1) for i in range(half, parts)):
        key_grads = unpack(back(2, indices), key_grads, width, local_heads, indices[0] * size)
    return tuple(g[None] for g in tuple(query_grads) + tuple(key_grads)) + (gain_grad,)


def solution(mesh):
    tokens = P("dp", "ctx", None)
    return jax.shard_map(
        per_device,
        mesh=mesh,
        in_specs=(tokens,) * 6 + (P(),) + (tokens,) * 2,
        out_specs=(tokens,) * 6 + (P("ctx"),),
        check_vma=False,
    )
```

```python
import functools
import math

import jax
import jax.numpy as jnp
from jax import lax
from jax.experimental import pallas as pl
from jax.experimental.pallas import tpu as pltpu
from jax.sharding import PartitionSpec as P

HEAD_DIM = 128
MEMBERS = 4
F32 = jnp.float32
BF16 = jnp.bfloat16


def dot(left, right, left_dim, right_dim):
    return lax.dot_general(
        left, right, (((left_dim,), (right_dim,)), ((), ())), preferred_element_type=F32
    )


def pack_kernel(table_ref, *refs):
    ins, outs = refs[: 4 * MEMBERS], refs[4 * MEMBERS :]
    for j, out_ref in enumerate(outs):
        for h in range(out_ref.shape[0]):
            for i, ref in enumerate(ins[4 * j : 4 * j + 4]):
                out_ref[h, :, i * HEAD_DIM : (i + 1) * HEAD_DIM] = ref[
                    :, h * HEAD_DIM : (h + 1) * HEAD_DIM
                ]


def pack(table, arrays, local_heads, first, count):
    rows = arrays[0].shape[0]
    block = math.gcd(count, first, 2)
    steps = count // block

    def columns(j):
        return pl.BlockSpec(
            (rows, block * HEAD_DIM),
            lambda i, table_ref: (0, (table_ref[j] * local_heads + first) // block + i),
        )

    return pl.pallas_call(
        pack_kernel,
        grid_spec=pltpu.PrefetchScalarGridSpec(
            num_scalar_prefetch=1,
            grid=(steps,),
            in_specs=[columns(j) for j in range(MEMBERS) for _ in range(4)],
            out_specs=[
                pl.BlockSpec((block, rows, 4 * HEAD_DIM), lambda i, table_ref: (i, 0, 0))
            ]
            * MEMBERS,
        ),
        out_shape=[jax.ShapeDtypeStruct((count, rows, 4 * HEAD_DIM), BF16)] * MEMBERS,
        cost_estimate=pl.CostEstimate(
            flops=0, bytes_accessed=MEMBERS * count * rows * HEAD_DIM * 16, transcendentals=0
        ),
    )(table, *(list(arrays) * MEMBERS))


def unpack_kernel(terms, results, table_ref, *refs):
    outs = refs[-results:]
    for j in range(MEMBERS):

        @pl.when(pl.program_id(0) == j)
        def _(j=j):
            total = refs[j][...].astype(F32)
            for t in range(1, terms):
                total = total + refs[t * MEMBERS + j][...].astype(F32)
            for h in range(total.shape[0]):
                for i, ref in enumerate(outs):
                    ref[:, h * HEAD_DIM : (h + 1) * HEAD_DIM] = total[
                        h, :, i * HEAD_DIM : (i + 1) * HEAD_DIM
                    ].astype(BF16)


def unpack(table, pieces, before, width, local_heads, first):
    terms = len(pieces) // MEMBERS
    count, rows, lanes = pieces[0].shape
    results = lanes // HEAD_DIM
    old = list(before or ())
    return pl.pallas_call(
        functools.partial(unpack_kernel, terms, results),
        grid_spec=pltpu.PrefetchScalarGridSpec(
            num_scalar_prefetch=1,
            grid=(MEMBERS,),
            in_specs=[pl.BlockSpec((count, rows, lanes), lambda j, table_ref: (0, 0, 0))]
            * len(pieces)
            + [pl.BlockSpec(memory_space=pl.ANY)] * len(old),
            out_specs=[
                pl.BlockSpec(
                    (rows, count * HEAD_DIM),
                    lambda j, table_ref: (0, (table_ref[j] * local_heads + first) // count),
                )
            ]
            * results,
        ),
        out_shape=[jax.ShapeDtypeStruct((rows, width), BF16)] * results,
        input_output_aliases={1 + len(pieces) + i: i for i in range(len(old))},
        compiler_params=pltpu.CompilerParams(vmem_limit_bytes=32 * 1024 * 1024),
        cost_estimate=pl.CostEstimate(
            flops=0, bytes_accessed=count * rows * lanes * MEMBERS * 8, transcendentals=0
        ),
    )(table, *pieces, *old)


def attention_kernel(pieces, scale, table_ref, gain_ref, *refs):
    row_refs, key_refs = refs[:MEMBERS], refs[MEMBERS : MEMBERS + pieces]
    outs = refs[MEMBERS + pieces :]
    gain_out, dq_refs, key_outs = outs[0], outs[1 : 1 + MEMBERS], outs[1 + MEMBERS :]
    d = HEAD_DIM
    part_rows, key_rows = row_refs[0].shape[1], key_refs[0].shape[1]
    every = jnp.concatenate([ref[0] for ref in key_refs], axis=0)
    k, k_kt = every[:, :d], every[:, : 2 * d]
    v, v_vt = every[:, 2 * d : 3 * d], every[:, 2 * d :]
    gain = gain_ref[...].astype(F32)
    sums = None
    for start in range(0, MEMBERS, 2):
        rows = jnp.concatenate([row_refs[start][0], row_refs[start + 1][0]], axis=0)
        q, qt = rows[:, :d], rows[:, d : 2 * d]
        gy = rows[:, 2 * d : 3 * d].astype(F32)
        gyt = rows[:, 3 * d :].astype(F32)
        go = (gy * gain).astype(BF16)
        got = (gyt * gain).astype(BF16)
        go_got = jnp.concatenate([go, got], axis=1)

        scores = dot(q, k, 1, 1) * scale
        scores_tan = dot(jnp.concatenate([qt, q], axis=1), k_kt, 1, 1) * scale
        d_probs = dot(go_got, v_vt, 1, 1)
        d_probs_tan = dot(got, v, 1, 1)
        top = jnp.max(scores, axis=-1, keepdims=True)
        raised = jnp.exp(scores - top)
        probs = raised * (1.0 / jnp.sum(raised, axis=-1, keepdims=True))
        offset = jnp.sum(probs * scores_tan, axis=-1, keepdims=True)
        centred = scores_tan - offset
        p_low = probs.astype(BF16)
        pt_low = (probs * centred).astype(BF16)
        inner = jnp.sum(probs * d_probs_tan, axis=-1, keepdims=True)
        dst_low = (probs * (d_probs_tan - inner)).astype(BF16)
        totals = d_probs + d_probs_tan * centred - inner * scores_tan
        ds = probs * (totals - jnp.sum(probs * totals, axis=-1, keepdims=True))
        ds_low = ds.astype(BF16)

        out_pair = dot(p_low, v_vt, 1, 0)
        attn_out = out_pair[:, :d].astype(BF16).astype(F32)
        attn_tan = (dot(pt_low, v, 1, 0) + out_pair[:, d:]).astype(BF16).astype(F32)
        gain_sum = jnp.sum(gy * attn_out + gyt * attn_tan, axis=0, keepdims=True)
        q_pair = dot(dst_low, k_kt, 1, 0)
        dq = scale * (dot(ds_low, k, 1, 0) + q_pair[:, d:])
        dqt = scale * q_pair[:, :d]
        both = jnp.concatenate([dq, dqt], axis=1).astype(BF16)
        dq_refs[start][0] = both[:part_rows]
        dq_refs[start + 1][0] = both[part_rows:]

        k_pair = dot(dst_low, rows[:, : 2 * d], 0, 0)
        v_pair = dot(p_low, go_got, 0, 0)
        terms = (
            dot(ds_low, q, 0, 0) + k_pair[:, d:],
            k_pair[:, :d],
            v_pair[:, :d] + dot(pt_low, got, 0, 0),
            v_pair[:, d:],
            gain_sum,
        )
        sums = terms if sums is None else tuple(a + b for a, b in zip(sums, terms))
    dk, dkt, dv, dvt, gain_sum = sums
    gain_out[0] = gain_sum
    for i, part in enumerate((scale * dk, scale * dkt, dv, dvt)):
        columns = slice(i * d, (i + 1) * d)
        for p, ref in enumerate(key_outs):
            ref[0, :, columns] = part[p * key_rows : (p + 1) * key_rows].astype(ref.dtype)


def attention(table, gain, rows, keys, local_heads, first, count):
    part_rows, key_rows = rows[0].shape[1], keys[0].shape[1]
    d = HEAD_DIM

    def spec(rows_of, lanes):
        return pl.BlockSpec((1, rows_of, lanes), lambda h, table_ref: (h, 0, 0))

    pairs = count * MEMBERS * part_rows * len(keys) * key_rows
    return pl.pallas_call(
        functools.partial(attention_kernel, len(keys), 1.0 / math.sqrt(d)),
        grid_spec=pltpu.PrefetchScalarGridSpec(
            num_scalar_prefetch=1,
            grid=(count,),
            in_specs=[
                pl.BlockSpec(
                    (1, d), lambda h, table_ref: (0, table_ref[0] * local_heads + first + h)
                )
            ]
            + [spec(part_rows, 4 * d)] * MEMBERS
            + [spec(key_rows, 4 * d)] * len(keys),
            out_specs=[spec(1, d)]
            + [spec(part_rows, 2 * d)] * MEMBERS
            + [spec(key_rows, 4 * d)] * len(keys),
        ),
        out_shape=[jax.ShapeDtypeStruct((count, 1, d), F32)]
        + [jax.ShapeDtypeStruct((count, part_rows, 2 * d), BF16)] * MEMBERS
        + [jax.ShapeDtypeStruct((count, key_rows, 4 * d), F32)]
        + [jax.ShapeDtypeStruct((count, key_rows, 4 * d), BF16)] * (len(keys) - 1),
        compiler_params=pltpu.CompilerParams(vmem_limit_bytes=48 * 1024 * 1024),
        cost_estimate=pl.CostEstimate(
            flops=pairs * 36 * d, bytes_accessed=pairs * 8, transcendentals=pairs
        ),
    )(table, gain, *rows, *keys)


def sum_over(array, axis):
    size = lax.axis_size(axis)
    if size & (size - 1):
        return lax.psum(array, axis)
    far = 1
    while far < size:
        array = array + lax.ppermute(array, axis, [(i, i ^ far) for i in range(size)])
        far *= 2
    return array


def per_device(
    queries, query_tangent, keys, key_tangent, values, value_tangent, out_gain, grad_y, grad_y_tan
):
    count = lax.axis_size("ctx")
    groups = count // MEMBERS
    width = queries.shape[2]
    local_heads = width // HEAD_DIM // MEMBERS
    place = lax.axis_index("ctx")
    member, group = lax.rem(place, MEMBERS), place // MEMBERS
    table = jnp.stack([member ^ j for j in range(MEMBERS)]).astype(jnp.int32)

    def send(array, far, j):
        pairs = [(i, (i + far * MEMBERS) % count ^ j) for i in range(count)]
        return array if far == 0 and j == 0 else lax.ppermute(array, "ctx", pairs)

    rows_in = (queries[0], query_tangent[0], grad_y[0], grad_y_tan[0])
    key_in = (keys[0], key_tangent[0], values[0], value_tangent[0])
    gain = out_gain.reshape(1, width)
    half = max(1, local_heads // 2)
    firsts = tuple(range(0, local_heads, half))

    keys_of, rows_of = [], []
    for first in firsts:
        packed = pack(table, key_in, local_heads, first, half)
        far_keys = [
            send(packed[j], far, j) for far in range(1, groups) for j in range(MEMBERS)
        ]
        keys_of.append([send(packed[j], 0, j) for j in range(MEMBERS)] + far_keys)
        packed = pack(table, rows_in, local_heads, first, half)
        rows_of.append([send(packed[j], 0, j) for j in range(MEMBERS)])

    outs = []
    query_grads = key_grads = None
    for first, rows, keys_here in zip(firsts, rows_of, keys_of):
        out = attention(table, gain, rows, keys_here, local_heads, first, half)
        outs.append(out)
        grads = out[1 + MEMBERS :]
        far_back = [
            send(grads[far * MEMBERS + j], -far, j)
            for far in range(1, groups)
            for j in range(MEMBERS)
        ]
        back = [send(grads[j], 0, j) for j in range(MEMBERS)] + far_back
        key_grads = unpack(table, back, key_grads, width, local_heads, first)
        back = [send(out[1 + j], 0, j) for j in range(MEMBERS)]
        query_grads = unpack(table, back, query_grads, width, local_heads, first)

    gain_mine = jnp.concatenate([out[0] for out in outs]).reshape(-1)
    gain_mine = sum_over(gain_mine, "dp")
    gain_all = gain_mine
    for far in range(1, groups):
        gain_all = gain_all + send(gain_mine, far, 0)
    gain_part = lax.dynamic_slice_in_dim(gain_all, group * (width // count), width // count)
    gain_grad = lax.ppermute(
        gain_part,
        "ctx",
        [(g * MEMBERS + r, r * groups + g) for g in range(groups) for r in range(MEMBERS)],
    )
    return tuple(g[None] for g in tuple(query_grads) + tuple(key_grads)) + (gain_grad,)


def solution(mesh):
    tokens = P("dp", "ctx", None)
    return jax.shard_map(
        per_device,
        mesh=mesh,
        in_specs=(tokens,) * 6 + (P(),) + (tokens,) * 2,
        out_specs=(tokens,) * 6 + (P("ctx"),),
        check_vma=False,
    )
```

```python
import functools
import math

import jax
import jax.numpy as jnp
from jax import lax
from jax.experimental import pallas as pl
from jax.experimental.pallas import tpu as pltpu
from jax.sharding import PartitionSpec as P

HEAD_DIM = 128
MEMBERS = 4
DEPTH = 5
F32 = jnp.float32
BF16 = jnp.bfloat16


def dot(left, right, left_dim, right_dim):
    return lax.dot_general(
        left, right, (((left_dim,), (right_dim,)), ((), ())), preferred_element_type=F32
    )


def pack_kernel(groups_of_refs, table_ref, *refs):
    ins, outs = refs[: -MEMBERS], refs[-MEMBERS:]
    each = 4 * groups_of_refs
    for j, out_ref in enumerate(outs):
        for h in range(out_ref.shape[0]):
            row = 0
            for n, ref in enumerate(ins[each * j : each * (j + 1)]):
                i = n % 4
                out_ref[h, row : row + ref.shape[0], i * HEAD_DIM : (i + 1) * HEAD_DIM] = ref[
                    :, h * HEAD_DIM : (h + 1) * HEAD_DIM
                ]
                if i == 3:
                    row += ref.shape[0]


def pack(table, arrays, local_heads, first, count):
    rows = sum(a.shape[0] for a in arrays) // 4
    block = math.gcd(count, first, 2)
    steps = count // block

    def columns(array, j):
        return pl.BlockSpec(
            (array.shape[0], block * HEAD_DIM),
            lambda i, table_ref: (0, (table_ref[j] * local_heads + first) // block + i),
        )

    return pl.pallas_call(
        functools.partial(pack_kernel, len(arrays) // 4),
        grid_spec=pltpu.PrefetchScalarGridSpec(
            num_scalar_prefetch=1,
            grid=(steps,),
            in_specs=[columns(a, j) for j in range(MEMBERS) for a in arrays],
            out_specs=[
                pl.BlockSpec((block, rows, 4 * HEAD_DIM), lambda i, table_ref: (i, 0, 0))
            ]
            * MEMBERS,
        ),
        out_shape=[jax.ShapeDtypeStruct((count, rows, 4 * HEAD_DIM), BF16)] * MEMBERS,
        compiler_params=pltpu.CompilerParams(vmem_limit_bytes=32 * 1024 * 1024),
        cost_estimate=pl.CostEstimate(
            flops=0, bytes_accessed=MEMBERS * count * rows * HEAD_DIM * 16, transcendentals=0
        ),
    )(table, *(list(arrays) * MEMBERS))


def unpack_kernel(pieces, table_ref, *refs):
    outs = refs[-6:]
    key_rows, half_rows = outs[0].shape[0], outs[4].shape[0] // 2
    d = HEAD_DIM
    for j in range(MEMBERS):

        @pl.when(pl.program_id(0) == j)
        def _(j=j):
            near = refs[j]
            total = near[:, :key_rows].astype(F32)
            for p in range(MEMBERS + j, pieces, MEMBERS):
                total = total + refs[p][...].astype(F32)
            for h in range(total.shape[0]):
                columns = slice(h * d, (h + 1) * d)
                for i, ref in enumerate(outs[:4]):
                    ref[:, columns] = total[h, :, i * d : (i + 1) * d].astype(BF16)
                for i, ref in enumerate(outs[4:]):
                    ref[:half_rows, columns] = near[h, key_rows:, i * d : (i + 1) * d]
                    ref[half_rows:, columns] = near[h, key_rows:, (i + 2) * d : (i + 3) * d]


def unpack(table, pieces, before, rows_q, rows_k, width, local_heads, first):
    count, lanes = pieces[0].shape[0], 4 * HEAD_DIM
    old = list(before or ())
    rows_of = [rows_k] * 4 + [rows_q] * 2
    return pl.pallas_call(
        functools.partial(unpack_kernel, len(pieces)),
        grid_spec=pltpu.PrefetchScalarGridSpec(
            num_scalar_prefetch=1,
            grid=(MEMBERS,),
            in_specs=[
                pl.BlockSpec((count, p.shape[1], lanes), lambda j, table_ref: (0, 0, 0))
                for p in pieces
            ]
            + [pl.BlockSpec(memory_space=pl.ANY)] * len(old),
            out_specs=[
                pl.BlockSpec(
                    (rows, count * HEAD_DIM),
                    lambda j, table_ref: (0, (table_ref[j] * local_heads + first) // count),
                )
                for rows in rows_of
            ],
        ),
        out_shape=[jax.ShapeDtypeStruct((rows, width), BF16) for rows in rows_of],
        input_output_aliases={1 + len(pieces) + i: i for i in range(len(old))},
        compiler_params=pltpu.CompilerParams(vmem_limit_bytes=32 * 1024 * 1024),
        cost_estimate=pl.CostEstimate(
            flops=0, bytes_accessed=count * rows_k * lanes * MEMBERS * 16, transcendentals=0
        ),
    )(table, *pieces, *old)


def attention_kernel(pieces, key_rows, scale, table_ref, gain_ref, *refs):
    near_refs, far_refs = refs[:MEMBERS], refs[MEMBERS:pieces]
    gain_out, key_outs = refs[pieces], refs[pieces + 1 :]
    d = HEAD_DIM
    part_rows = near_refs[0].shape[1] - key_rows
    every = jnp.concatenate(
        [ref[0, :key_rows] for ref in near_refs] + [ref[0] for ref in far_refs], axis=0
    )
    k, k_kt = every[:, :d], every[:, : 2 * d]
    v, v_vt = every[:, 2 * d : 3 * d], every[:, 2 * d :]
    gain = gain_ref[...].astype(F32)
    sums = None
    for start in range(0, MEMBERS, 2):
        rows = jnp.concatenate(
            [near_refs[start][0, key_rows:], near_refs[start + 1][0, key_rows:]], axis=0
        )
        q, qt = rows[:, :d], rows[:, d : 2 * d]
        gy = rows[:, 2 * d : 3 * d].astype(F32)
        gyt = rows[:, 3 * d :].astype(F32)
        go = (gy * gain).astype(BF16)
        got = (gyt * gain).astype(BF16)
        go_got = jnp.concatenate([go, got], axis=1)

        scores = dot(q, k, 1, 1) * scale
        scores_tan = dot(jnp.concatenate([qt, q], axis=1), k_kt, 1, 1) * scale
        d_probs = dot(go_got, v_vt, 1, 1)
        d_probs_tan = dot(got, v, 1, 1)
        top = jnp.max(scores, axis=-1, keepdims=True)
        raised = jnp.exp(scores - top)
        probs = raised * (1.0 / jnp.sum(raised, axis=-1, keepdims=True))
        offset = jnp.sum(probs * scores_tan, axis=-1, keepdims=True)
        centred = scores_tan - offset
        p_low = probs.astype(BF16)
        pt_low = (probs * centred).astype(BF16)
        inner = jnp.sum(probs * d_probs_tan, axis=-1, keepdims=True)
        dst_low = (probs * (d_probs_tan - inner)).astype(BF16)
        totals = d_probs + d_probs_tan * centred - inner * scores_tan
        ds = probs * (totals - jnp.sum(probs * totals, axis=-1, keepdims=True))
        ds_low = ds.astype(BF16)

        out_pair = dot(p_low, v_vt, 1, 0)
        attn_out = out_pair[:, :d].astype(BF16).astype(F32)
        attn_tan = (dot(pt_low, v, 1, 0) + out_pair[:, d:]).astype(BF16).astype(F32)
        gain_sum = jnp.sum(gy * attn_out + gyt * attn_tan, axis=0, keepdims=True)
        q_pair = dot(dst_low, k_kt, 1, 0)
        dq = scale * (dot(ds_low, k, 1, 0) + q_pair[:, d:])
        dqt = scale * q_pair[:, :d]
        both = jnp.concatenate([dq, dqt], axis=1).astype(BF16)
        for n in range(4):
            key_outs[start + n // 2][0, key_rows:, (n % 2) * 2 * d : (n % 2 + 1) * 2 * d] = both[
                n * part_rows // 2 : (n + 1) * part_rows // 2
            ]

        k_pair = dot(dst_low, rows[:, : 2 * d], 0, 0)
        v_pair = dot(p_low, go_got, 0, 0)
        terms = (
            dot(ds_low, q, 0, 0) + k_pair[:, d:],
            k_pair[:, :d],
            v_pair[:, :d] + dot(pt_low, got, 0, 0),
            v_pair[:, d:],
            gain_sum,
        )
        sums = terms if sums is None else tuple(a + b for a, b in zip(sums, terms))
    dk, dkt, dv, dvt, gain_sum = sums
    gain_out[0] = gain_sum
    for i, part in enumerate((scale * dk, scale * dkt, dv, dvt)):
        columns = slice(i * d, (i + 1) * d)
        for p, ref in enumerate(key_outs):
            ref[0, :key_rows, columns] = part[p * key_rows : (p + 1) * key_rows].astype(ref.dtype)


def attention(table, gain, pieces, key_rows, local_heads, first, count):
    d = HEAD_DIM
    part_rows = pieces[0].shape[1] - key_rows
    home_rows = [key_rows + part_rows // 2] * MEMBERS
    home_rows += [key_rows] * (len(pieces) - MEMBERS)

    def spec(rows_of, lanes):
        return pl.BlockSpec((1, rows_of, lanes), lambda h, table_ref: (h, 0, 0))

    pairs = count * MEMBERS * part_rows * len(pieces) * key_rows
    return pl.pallas_call(
        functools.partial(attention_kernel, len(pieces), key_rows, 1.0 / math.sqrt(d)),
        grid_spec=pltpu.PrefetchScalarGridSpec(
            num_scalar_prefetch=1,
            grid=(count,),
            in_specs=[
                pl.BlockSpec(
                    (1, d), lambda h, table_ref: (0, table_ref[0] * local_heads + first + h)
                )
            ]
            + [spec(p.shape[1], 4 * d) for p in pieces],
            out_specs=[spec(1, d)] + [spec(rows, 4 * d) for rows in home_rows],
        ),
        out_shape=[jax.ShapeDtypeStruct((count, 1, d), F32)]
        + [jax.ShapeDtypeStruct((count, rows, 4 * d), BF16) for rows in home_rows],
        compiler_params=pltpu.CompilerParams(vmem_limit_bytes=48 * 1024 * 1024),
        cost_estimate=pl.CostEstimate(
            flops=pairs * 36 * d, bytes_accessed=pairs * 8, transcendentals=pairs
        ),
    )(table, gain, *pieces)


def after(array, *before):
    return lax.optimization_barrier((array,) + before)[0] if before else array


def sum_over(array, axis):
    size = lax.axis_size(axis)
    if size & (size - 1):
        return lax.psum(array, axis)
    far = 1
    while far < size:
        array = array + lax.ppermute(array, axis, [(i, i ^ far) for i in range(size)])
        far *= 2
    return array


def per_device(
    queries, query_tangent, keys, key_tangent, values, value_tangent, out_gain, grad_y, grad_y_tan
):
    count = lax.axis_size("ctx")
    groups = count // MEMBERS
    width = queries.shape[2]
    local_heads = width // HEAD_DIM // MEMBERS
    place = lax.axis_index("ctx")
    member, group = lax.rem(place, MEMBERS), place // MEMBERS
    table = jnp.stack([member ^ j for j in range(MEMBERS)]).astype(jnp.int32)

    rows_in = (queries[0], query_tangent[0], grad_y[0], grad_y_tan[0])
    key_in = (keys[0], key_tangent[0], values[0], value_tangent[0])
    rows_q, rows_k = rows_in[0].shape[0], key_in[0].shape[0]
    gain = out_gain.reshape(1, width)
    half = max(1, local_heads // 2)
    firsts = (0, half)
    flow = []

    def send(array, far, j):
        if far == 0 and j == 0:
            return array
        pairs = [(i, (i + far * MEMBERS) % count ^ j) for i in range(count)]
        if len(flow) >= DEPTH:
            array = after(array, flow[-DEPTH])
        flow.append(lax.ppermute(array, "ctx", pairs))
        return flow[-1]

    def spread(near, far_pieces, sign):
        near, far_pieces = list(near), list(far_pieces)
        order = (2, 3, 1, 0)
        for n, j in enumerate(order):
            for far in range(1, groups):
                p = (far - 1) * MEMBERS + n
                far_pieces[p] = send(far_pieces[p], sign * far, n)
            near[j] = send(near[j], 0, j)
        return near + far_pieces

    def outward(first, *before):
        arrays = (after(key_in[0], *before),) + key_in[1:]
        far_pieces = pack(table, arrays, local_heads, first, half)
        near = pack(table, arrays + rows_in, local_heads, first, half)
        return spread(near, list(far_pieces) * (groups - 1), 1)

    def attend(first, pieces, *before):
        pieces = [after(pieces[0], *before)] + pieces[1:]
        out = attention(table, gain, pieces, rows_k, local_heads, first, half)
        return out[0], out[1 : 1 + MEMBERS], out[1 + MEMBERS :]

    pieces0 = outward(firsts[0])
    pieces1 = outward(firsts[1])
    out0 = attend(firsts[0], pieces0)
    back0 = spread(out0[1], out0[2], -1)
    out1 = attend(firsts[1], pieces1, back0[MEMBERS])
    back1 = spread(out1[1], out1[2], -1)
    gain_mine = jnp.concatenate([out0[0], out1[0]]).reshape(groups, width // count)
    gain_part = 0.0
    for far in range(groups):
        whose = lax.rem(group + far, groups)
        piece = lax.dynamic_slice_in_dim(gain_mine, whose, 1)[0]
        pairs = [
            (g * MEMBERS + r, r * groups + (g + far) % groups)
            for g in range(groups)
            for r in range(MEMBERS)
        ]
        gain_part = gain_part + lax.ppermute(piece, "ctx", pairs)
    gain_grad = sum_over(after(gain_part, back1[MEMBERS]), "dp")
    grads = unpack(table, back0, None, rows_q, rows_k, width, local_heads, firsts[0])
    grads = unpack(table, back1, grads, rows_q, rows_k, width, local_heads, firsts[1])
    return tuple(g[None] for g in tuple(grads[4:]) + tuple(grads[:4])) + (gain_grad,)


def solution(mesh):
    tokens = P("dp", "ctx", None)
    return jax.shard_map(
        per_device,
        mesh=mesh,
        in_specs=(tokens,) * 6 + (P(),) + (tokens,) * 2,
        out_specs=(tokens,) * 6 + (P("ctx"),),
        check_vma=False,
    )
```

```python
import functools
import math

import jax
import jax.numpy as jnp
from jax import lax
from jax.experimental import pallas as pl
from jax.experimental.pallas import tpu as pltpu
from jax.sharding import PartitionSpec as P

HEAD_DIM = 128
MEMBERS = 4
DEPTH = 5
ORDER = ((True, 0), (False, 2), (True, 1), (False, 3), (True, 2), (False, 1), (True, 3))
VMEM = 60 * 1024 * 1024
F32 = jnp.float32
BF16 = jnp.bfloat16


def dot(left, right, left_dim, right_dim):
    return lax.dot_general(
        left, right, (((left_dim,), (right_dim,)), ((), ())), preferred_element_type=F32
    )


def pack_kernel(groups_of_refs, table_ref, *refs):
    ins, outs = refs[: -MEMBERS], refs[-MEMBERS:]
    each = 4 * groups_of_refs
    for j, out_ref in enumerate(outs):
        for h in range(out_ref.shape[0]):
            row = 0
            for n, ref in enumerate(ins[each * j : each * (j + 1)]):
                i = n % 4
                out_ref[h, row : row + ref.shape[0], i * HEAD_DIM : (i + 1) * HEAD_DIM] = ref[
                    :, h * HEAD_DIM : (h + 1) * HEAD_DIM
                ]
                if i == 3:
                    row += ref.shape[0]


def pack(table, arrays, local_heads, first, count, vmem):
    rows = sum(a.shape[0] for a in arrays) // 4
    block = math.gcd(count, first, 2)
    steps = count // block

    def columns(array, j):
        return pl.BlockSpec(
            (array.shape[0], block * HEAD_DIM),
            lambda i, table_ref: (0, (table_ref[j] * local_heads + first) // block + i),
        )

    return pl.pallas_call(
        functools.partial(pack_kernel, len(arrays) // 4),
        grid_spec=pltpu.PrefetchScalarGridSpec(
            num_scalar_prefetch=1,
            grid=(steps,),
            in_specs=[columns(a, j) for j in range(MEMBERS) for a in arrays],
            out_specs=[
                pl.BlockSpec((block, rows, 4 * HEAD_DIM), lambda i, table_ref: (i, 0, 0))
            ]
            * MEMBERS,
        ),
        out_shape=[jax.ShapeDtypeStruct((count, rows, 4 * HEAD_DIM), BF16)] * MEMBERS,
        compiler_params=pltpu.CompilerParams(vmem_limit_bytes=vmem),
        cost_estimate=pl.CostEstimate(
            flops=0, bytes_accessed=MEMBERS * count * rows * HEAD_DIM * 16, transcendentals=0
        ),
    )(table, *(list(arrays) * MEMBERS))


def unpack_kernel(pieces, table_ref, *refs):
    outs = refs[-6:]
    key_rows, half_rows = outs[0].shape[0], outs[4].shape[0] // 2
    d = HEAD_DIM
    for j in range(MEMBERS):

        @pl.when(pl.program_id(0) == j)
        def _(j=j):
            near = refs[j]
            total = near[:, :key_rows].astype(F32)
            for p in range(MEMBERS + j, pieces, MEMBERS):
                total = total + refs[p][...].astype(F32)
            for h in range(total.shape[0]):
                columns = slice(h * d, (h + 1) * d)
                for i, ref in enumerate(outs[:4]):
                    ref[:, columns] = total[h, :, i * d : (i + 1) * d].astype(BF16)
                for i, ref in enumerate(outs[4:]):
                    ref[:half_rows, columns] = near[h, key_rows:, i * d : (i + 1) * d]
                    ref[half_rows:, columns] = near[h, key_rows:, (i + 2) * d : (i + 3) * d]


def unpack(table, pieces, before, rows_q, rows_k, width, local_heads, first):
    count, lanes = pieces[0].shape[0], 4 * HEAD_DIM
    old = list(before or ())
    rows_of = [rows_k] * 4 + [rows_q] * 2
    return pl.pallas_call(
        functools.partial(unpack_kernel, len(pieces)),
        grid_spec=pltpu.PrefetchScalarGridSpec(
            num_scalar_prefetch=1,
            grid=(MEMBERS,),
            in_specs=[
                pl.BlockSpec((count, p.shape[1], lanes), lambda j, table_ref: (0, 0, 0))
                for p in pieces
            ]
            + [pl.BlockSpec(memory_space=pl.ANY)] * len(old),
            out_specs=[
                pl.BlockSpec(
                    (rows, count * HEAD_DIM),
                    lambda j, table_ref: (0, (table_ref[j] * local_heads + first) // count),
                )
                for rows in rows_of
            ],
        ),
        out_shape=[jax.ShapeDtypeStruct((rows, width), BF16) for rows in rows_of],
        input_output_aliases={1 + len(pieces) + i: i for i in range(len(old))},
        compiler_params=pltpu.CompilerParams(vmem_limit_bytes=VMEM // 2),
        cost_estimate=pl.CostEstimate(
            flops=0, bytes_accessed=count * rows_k * lanes * MEMBERS * 16, transcendentals=0
        ),
    )(table, *pieces, *old)


def attention_kernel(pieces, key_rows, scale, table_ref, gain_ref, *refs):
    near_refs, far_refs = refs[:MEMBERS], refs[MEMBERS:pieces]
    gain_out, key_outs = refs[pieces], refs[pieces + 1 :]
    d = HEAD_DIM
    part_rows = near_refs[0].shape[1] - key_rows
    every = jnp.concatenate(
        [ref[0, :key_rows] for ref in near_refs] + [ref[0] for ref in far_refs], axis=0
    )
    k, k_kt = every[:, :d], every[:, : 2 * d]
    v, v_vt = every[:, 2 * d : 3 * d], every[:, 2 * d :]
    gain = gain_ref[...].astype(F32)
    sums = None
    for start in range(0, MEMBERS, 2):
        rows = jnp.concatenate(
            [near_refs[start][0, key_rows:], near_refs[start + 1][0, key_rows:]], axis=0
        )
        q, qt = rows[:, :d], rows[:, d : 2 * d]
        gy = rows[:, 2 * d : 3 * d].astype(F32)
        gyt = rows[:, 3 * d :].astype(F32)
        go = (gy * gain).astype(BF16)
        got = (gyt * gain).astype(BF16)
        go_got = jnp.concatenate([go, got], axis=1)

        scores = dot(q, k, 1, 1) * scale
        scores_tan = dot(jnp.concatenate([qt, q], axis=1), k_kt, 1, 1) * scale
        d_probs = dot(go_got, v_vt, 1, 1)
        d_probs_tan = dot(got, v, 1, 1)
        top = jnp.max(scores, axis=-1, keepdims=True)
        raised = jnp.exp(scores - top)
        probs = raised * (1.0 / jnp.sum(raised, axis=-1, keepdims=True))
        offset = jnp.sum(probs * scores_tan, axis=-1, keepdims=True)
        centred = scores_tan - offset
        p_low = probs.astype(BF16)
        pt_low = (probs * centred).astype(BF16)
        inner = jnp.sum(probs * d_probs_tan, axis=-1, keepdims=True)
        dst_low = (probs * (d_probs_tan - inner)).astype(BF16)
        totals = d_probs + d_probs_tan * centred - inner * scores_tan
        ds = probs * (totals - jnp.sum(probs * totals, axis=-1, keepdims=True))
        ds_low = ds.astype(BF16)

        out_pair = dot(p_low, v_vt, 1, 0)
        attn_out = out_pair[:, :d].astype(BF16).astype(F32)
        attn_tan = (dot(pt_low, v, 1, 0) + out_pair[:, d:]).astype(BF16).astype(F32)
        gain_sum = jnp.sum(gy * attn_out + gyt * attn_tan, axis=0, keepdims=True)
        q_pair = dot(dst_low, k_kt, 1, 0)
        dq = scale * (dot(ds_low, k, 1, 0) + q_pair[:, d:])
        dqt = scale * q_pair[:, :d]
        both = jnp.concatenate([dq, dqt], axis=1).astype(BF16)
        for n in range(4):
            key_outs[start + n // 2][0, key_rows:, (n % 2) * 2 * d : (n % 2 + 1) * 2 * d] = both[
                n * part_rows // 2 : (n + 1) * part_rows // 2
            ]

        k_pair = dot(dst_low, rows[:, : 2 * d], 0, 0)
        v_pair = dot(p_low, go_got, 0, 0)
        terms = (
            dot(ds_low, q, 0, 0) + k_pair[:, d:],
            k_pair[:, :d],
            v_pair[:, :d] + dot(pt_low, got, 0, 0),
            v_pair[:, d:],
            gain_sum,
        )
        sums = terms if sums is None else tuple(a + b for a, b in zip(sums, terms))
    dk, dkt, dv, dvt, gain_sum = sums
    gain_out[0] = gain_sum
    for i, part in enumerate((scale * dk, scale * dkt, dv, dvt)):
        columns = slice(i * d, (i + 1) * d)
        for p, ref in enumerate(key_outs):
            ref[0, :key_rows, columns] = part[p * key_rows : (p + 1) * key_rows].astype(ref.dtype)


def attention(table, gain, pieces, key_rows, local_heads, first, count):
    d = HEAD_DIM
    part_rows = pieces[0].shape[1] - key_rows
    home_rows = [key_rows + part_rows // 2] * MEMBERS
    home_rows += [key_rows] * (len(pieces) - MEMBERS)

    def spec(rows_of, lanes):
        return pl.BlockSpec((1, rows_of, lanes), lambda h, table_ref: (h, 0, 0))

    pairs = count * MEMBERS * part_rows * len(pieces) * key_rows
    return pl.pallas_call(
        functools.partial(attention_kernel, len(pieces), key_rows, 1.0 / math.sqrt(d)),
        grid_spec=pltpu.PrefetchScalarGridSpec(
            num_scalar_prefetch=1,
            grid=(count,),
            in_specs=[
                pl.BlockSpec(
                    (1, d), lambda h, table_ref: (0, table_ref[0] * local_heads + first + h)
                )
            ]
            + [spec(p.shape[1], 4 * d) for p in pieces],
            out_specs=[spec(1, d)] + [spec(rows, 4 * d) for rows in home_rows],
        ),
        out_shape=[jax.ShapeDtypeStruct((count, 1, d), F32)]
        + [jax.ShapeDtypeStruct((count, rows, 4 * d), BF16) for rows in home_rows],
        compiler_params=pltpu.CompilerParams(vmem_limit_bytes=VMEM),
        cost_estimate=pl.CostEstimate(
            flops=pairs * 36 * d, bytes_accessed=pairs * 8, transcendentals=pairs
        ),
    )(table, gain, *pieces)


def after(array, *before):
    return lax.optimization_barrier((array,) + before)[0] if before else array


def per_device(
    queries, query_tangent, keys, key_tangent, values, value_tangent, out_gain, grad_y, grad_y_tan
):
    count = lax.axis_size("ctx")
    groups = count // MEMBERS
    width = queries.shape[2]
    local_heads = width // HEAD_DIM // MEMBERS
    place = lax.axis_index("ctx")
    member, group = lax.rem(place, MEMBERS), place // MEMBERS
    table = jnp.stack([member ^ j for j in range(MEMBERS)]).astype(jnp.int32)

    rows_in = (queries[0], query_tangent[0], grad_y[0], grad_y_tan[0])
    key_in = (keys[0], key_tangent[0], values[0], value_tangent[0])
    rows_q, rows_k = rows_in[0].shape[0], key_in[0].shape[0]
    gain = out_gain.reshape(1, width)
    half = max(1, local_heads // 2)
    firsts = (0, half)
    flow = []

    def send(array, far, j):
        if far == 0 and j == 0:
            return array
        pairs = [(i, (i + far * MEMBERS) % count ^ j) for i in range(count)]
        if len(flow) >= DEPTH:
            array = after(array, flow[-DEPTH])
        flow.append(lax.ppermute(array, "ctx", pairs))
        return flow[-1]

    def spread(near, far_pieces, sign, *before):
        near, far_pieces = list(near), list(far_pieces)
        for n, (is_far, j) in enumerate(ORDER):
            ready = before if n == 6 else ()
            if not is_far:
                near[j] = send(after(near[j], *ready), 0, j)
                continue
            for far in range(1, groups):
                p = (far - 1) * MEMBERS + j
                far_pieces[p] = send(after(far_pieces[p], *ready), sign * far, j)
        return near + far_pieces

    def outward(first, *before):
        arrays = (after(key_in[0], *before),) + key_in[1:]
        far_pieces = pack(
            table, arrays, local_heads, first, half, VMEM if first == 0 else VMEM // 2
        )
        near = pack(table, arrays + rows_in, local_heads, first, half, VMEM // 2)
        return spread(near, list(far_pieces) * (groups - 1), 1)

    def attend(first, pieces, *before):
        pieces = [after(pieces[0], *before)] + pieces[1:]
        out = attention(table, gain, pieces, rows_k, local_heads, first, half)
        return out[0], out[1 : 1 + MEMBERS], out[1 + MEMBERS :]

    pieces0 = outward(firsts[0])
    pieces1 = outward(firsts[1])
    out0 = attend(firsts[0], pieces0)
    back0 = spread(out0[1], out0[2], -1)
    out1 = attend(firsts[1], pieces1, back0[MEMBERS])
    grads = unpack(table, back0, None, rows_q, rows_k, width, local_heads, firsts[0])
    back1 = spread(out1[1], out1[2], -1, grads[0])
    gain_mine = jnp.concatenate([out0[0], out1[0]]).reshape(groups, width // count)
    gain_mine = lax.psum(gain_mine, "dp")
    gain_grad = 0.0
    for far in range(groups):
        whose = lax.rem(group + far, groups)
        piece = lax.dynamic_slice_in_dim(gain_mine, whose, 1)[0]
        pairs = [
            (g * MEMBERS + r, r * groups + (g + far) % groups)
            for g in range(groups)
            for r in range(MEMBERS)
        ]
        gain_grad = gain_grad + lax.ppermute(after(piece, flow[-6]), "ctx", pairs)
    grads = unpack(table, back1, grads, rows_q, rows_k, width, local_heads, firsts[1])
    return tuple(g[None] for g in tuple(grads[4:]) + tuple(grads[:4])) + (gain_grad,)


def solution(mesh):
    tokens = P("dp", "ctx", None)
    return jax.shard_map(
        per_device,
        mesh=mesh,
        in_specs=(tokens,) * 6 + (P(),) + (tokens,) * 2,
        out_specs=(tokens,) * 6 + (P("ctx"),),
        check_vma=False,
    )
```

```python
import functools
import math

import jax
import jax.numpy as jnp
from jax import lax
from jax.experimental import pallas as pl
from jax.experimental.pallas import tpu as pltpu
from jax.sharding import PartitionSpec as P

HEAD_DIM = 128
MEMBERS = 4
DEPTH = 5
ORDER = ((True, 0), (False, 3), (True, 1), (False, 2), (True, 3), (False, 1), (True, 2))
VMEM = 60 * 1024 * 1024
F32 = jnp.float32
BF16 = jnp.bfloat16


def dot(left, right, left_dim, right_dim):
    return lax.dot_general(
        left, right, (((left_dim,), (right_dim,)), ((), ())), preferred_element_type=F32
    )


def pack_kernel(groups_of_refs, table_ref, *refs):
    ins, outs = refs[: -MEMBERS], refs[-MEMBERS:]
    each = 4 * groups_of_refs
    for j, out_ref in enumerate(outs):
        for h in range(out_ref.shape[0]):
            row = 0
            for n, ref in enumerate(ins[each * j : each * (j + 1)]):
                i = n % 4
                out_ref[h, row : row + ref.shape[0], i * HEAD_DIM : (i + 1) * HEAD_DIM] = ref[
                    :, h * HEAD_DIM : (h + 1) * HEAD_DIM
                ]
                if i == 3:
                    row += ref.shape[0]


def pack(table, arrays, local_heads, first, count, vmem):
    rows = sum(a.shape[0] for a in arrays) // 4
    block = math.gcd(count, first, 2)
    steps = count // block

    def columns(array, j):
        return pl.BlockSpec(
            (array.shape[0], block * HEAD_DIM),
            lambda i, table_ref: (0, (table_ref[j] * local_heads + first) // block + i),
        )

    return pl.pallas_call(
        functools.partial(pack_kernel, len(arrays) // 4),
        grid_spec=pltpu.PrefetchScalarGridSpec(
            num_scalar_prefetch=1,
            grid=(steps,),
            in_specs=[columns(a, j) for j in range(MEMBERS) for a in arrays],
            out_specs=[
                pl.BlockSpec((block, rows, 4 * HEAD_DIM), lambda i, table_ref: (i, 0, 0))
            ]
            * MEMBERS,
        ),
        out_shape=[jax.ShapeDtypeStruct((count, rows, 4 * HEAD_DIM), BF16)] * MEMBERS,
        compiler_params=pltpu.CompilerParams(vmem_limit_bytes=vmem),
        cost_estimate=pl.CostEstimate(
            flops=0, bytes_accessed=MEMBERS * count * rows * HEAD_DIM * 16, transcendentals=0
        ),
    )(table, *(list(arrays) * MEMBERS))


def unpack_kernel(members, pieces, table_ref, *refs):
    outs = refs[-6:]
    key_rows, half_rows = outs[0].shape[0], outs[4].shape[0] // 2
    d = HEAD_DIM
    for j in range(members):

        @pl.when(pl.program_id(0) == j)
        def _(j=j):
            near = refs[j]
            total = near[:, :key_rows].astype(F32)
            for p in range(members + j, pieces, members):
                total = total + refs[p][...].astype(F32)
            for h in range(total.shape[0]):
                columns = slice(h * d, (h + 1) * d)
                for i, ref in enumerate(outs[:4]):
                    ref[:, columns] = total[h, :, i * d : (i + 1) * d].astype(BF16)
                for i, ref in enumerate(outs[4:]):
                    ref[:half_rows, columns] = near[h, key_rows:, i * d : (i + 1) * d]
                    ref[half_rows:, columns] = near[h, key_rows:, (i + 2) * d : (i + 3) * d]


def unpack(table, chosen, pieces, before, rows_q, rows_k, width, local_heads, first):
    count, lanes = pieces[0].shape[0], 4 * HEAD_DIM
    old = list(before or ())
    pieces = [p for n, p in enumerate(pieces) if n % MEMBERS in chosen]
    table = jnp.stack([table[j] for j in chosen])
    rows_of = [rows_k] * 4 + [rows_q] * 2
    return pl.pallas_call(
        functools.partial(unpack_kernel, len(chosen), len(pieces)),
        grid_spec=pltpu.PrefetchScalarGridSpec(
            num_scalar_prefetch=1,
            grid=(len(chosen),),
            in_specs=[
                pl.BlockSpec((count, p.shape[1], lanes), lambda j, table_ref: (0, 0, 0))
                for p in pieces
            ]
            + [pl.BlockSpec(memory_space=pl.ANY)] * len(old),
            out_specs=[
                pl.BlockSpec(
                    (rows, count * HEAD_DIM),
                    lambda j, table_ref: (0, (table_ref[j] * local_heads + first) // count),
                )
                for rows in rows_of
            ],
        ),
        out_shape=[jax.ShapeDtypeStruct((rows, width), BF16) for rows in rows_of],
        input_output_aliases={1 + len(pieces) + i: i for i in range(len(old))},
        compiler_params=pltpu.CompilerParams(vmem_limit_bytes=VMEM // 2),
        cost_estimate=pl.CostEstimate(
            flops=0, bytes_accessed=count * rows_k * lanes * MEMBERS * 16, transcendentals=0
        ),
    )(table, *pieces, *old)


def attention_kernel(pieces, key_rows, scale, table_ref, gain_ref, *refs):
    near_refs, far_refs = refs[:MEMBERS], refs[MEMBERS:pieces]
    gain_out, key_outs = refs[pieces], refs[pieces + 1 :]
    d = HEAD_DIM
    part_rows = near_refs[0].shape[1] - key_rows
    every = jnp.concatenate(
        [ref[0, :key_rows] for ref in near_refs] + [ref[0] for ref in far_refs], axis=0
    )
    k, k_kt = every[:, :d], every[:, : 2 * d]
    v, v_vt = every[:, 2 * d : 3 * d], every[:, 2 * d :]
    gain = gain_ref[...].astype(F32)
    sums = None
    for start in range(0, MEMBERS, 2):
        rows = jnp.concatenate(
            [near_refs[start][0, key_rows:], near_refs[start + 1][0, key_rows:]], axis=0
        )
        q, qt = rows[:, :d], rows[:, d : 2 * d]
        gy = rows[:, 2 * d : 3 * d].astype(F32)
        gyt = rows[:, 3 * d :].astype(F32)
        go = (gy * gain).astype(BF16)
        got = (gyt * gain).astype(BF16)
        go_got = jnp.concatenate([go, got], axis=1)

        scores = dot(q, k, 1, 1) * scale
        scores_tan = dot(jnp.concatenate([qt, q], axis=1), k_kt, 1, 1) * scale
        d_probs = dot(go_got, v_vt, 1, 1)
        d_probs_tan = dot(got, v, 1, 1)
        top = jnp.max(scores, axis=-1, keepdims=True)
        raised = jnp.exp(scores - top)
        probs = raised * (1.0 / jnp.sum(raised, axis=-1, keepdims=True))
        offset = jnp.sum(probs * scores_tan, axis=-1, keepdims=True)
        centred = scores_tan - offset
        p_low = probs.astype(BF16)
        pt_low = (probs * centred).astype(BF16)
        inner = jnp.sum(probs * d_probs_tan, axis=-1, keepdims=True)
        dst_low = (probs * (d_probs_tan - inner)).astype(BF16)
        totals = d_probs + d_probs_tan * centred - inner * scores_tan
        ds = probs * (totals - jnp.sum(probs * totals, axis=-1, keepdims=True))
        ds_low = ds.astype(BF16)

        out_pair = dot(p_low, v_vt, 1, 0)
        attn_out = out_pair[:, :d].astype(BF16).astype(F32)
        attn_tan = (dot(pt_low, v, 1, 0) + out_pair[:, d:]).astype(BF16).astype(F32)
        gain_sum = jnp.sum(gy * attn_out + gyt * attn_tan, axis=0, keepdims=True)
        q_pair = dot(dst_low, k_kt, 1, 0)
        dq = scale * (dot(ds_low, k, 1, 0) + q_pair[:, d:])
        dqt = scale * q_pair[:, :d]
        both = jnp.concatenate([dq, dqt], axis=1).astype(BF16)
        for n in range(4):
            key_outs[start + n // 2][0, key_rows:, (n % 2) * 2 * d : (n % 2 + 1) * 2 * d] = both[
                n * part_rows // 2 : (n + 1) * part_rows // 2
            ]

        k_pair = dot(dst_low, rows[:, : 2 * d], 0, 0)
        v_pair = dot(p_low, go_got, 0, 0)
        terms = (
            dot(ds_low, q, 0, 0) + k_pair[:, d:],
            k_pair[:, :d],
            v_pair[:, :d] + dot(pt_low, got, 0, 0),
            v_pair[:, d:],
            gain_sum,
        )
        sums = terms if sums is None else tuple(a + b for a, b in zip(sums, terms))
    dk, dkt, dv, dvt, gain_sum = sums
    gain_out[0] = gain_sum
    for i, part in enumerate((scale * dk, scale * dkt, dv, dvt)):
        columns = slice(i * d, (i + 1) * d)
        for p, ref in enumerate(key_outs):
            ref[0, :key_rows, columns] = part[p * key_rows : (p + 1) * key_rows].astype(ref.dtype)


def attention(table, gain, pieces, key_rows, local_heads, first, count):
    d = HEAD_DIM
    part_rows = pieces[0].shape[1] - key_rows
    home_rows = [key_rows + part_rows // 2] * MEMBERS
    home_rows += [key_rows] * (len(pieces) - MEMBERS)

    def spec(rows_of, lanes):
        return pl.BlockSpec((1, rows_of, lanes), lambda h, table_ref: (h, 0, 0))

    pairs = count * MEMBERS * part_rows * len(pieces) * key_rows
    return pl.pallas_call(
        functools.partial(attention_kernel, len(pieces), key_rows, 1.0 / math.sqrt(d)),
        grid_spec=pltpu.PrefetchScalarGridSpec(
            num_scalar_prefetch=1,
            grid=(count,),
            in_specs=[
                pl.BlockSpec(
                    (1, d), lambda h, table_ref: (0, table_ref[0] * local_heads + first + h)
                )
            ]
            + [spec(p.shape[1], 4 * d) for p in pieces],
            out_specs=[spec(1, d)] + [spec(rows, 4 * d) for rows in home_rows],
        ),
        out_shape=[jax.ShapeDtypeStruct((count, 1, d), F32)]
        + [jax.ShapeDtypeStruct((count, rows, 4 * d), BF16) for rows in home_rows],
        compiler_params=pltpu.CompilerParams(vmem_limit_bytes=VMEM),
        cost_estimate=pl.CostEstimate(
            flops=pairs * 36 * d, bytes_accessed=pairs * 8, transcendentals=pairs
        ),
    )(table, gain, *pieces)


def after(array, *before):
    return lax.optimization_barrier((array,) + before)[0] if before else array


def per_device(
    queries, query_tangent, keys, key_tangent, values, value_tangent, out_gain, grad_y, grad_y_tan
):
    count = lax.axis_size("ctx")
    groups = count // MEMBERS
    width = queries.shape[2]
    local_heads = width // HEAD_DIM // MEMBERS
    place = lax.axis_index("ctx")
    member, group = lax.rem(place, MEMBERS), place // MEMBERS
    table = jnp.stack([member ^ j for j in range(MEMBERS)]).astype(jnp.int32)

    rows_in = (queries[0], query_tangent[0], grad_y[0], grad_y_tan[0])
    key_in = (keys[0], key_tangent[0], values[0], value_tangent[0])
    rows_q, rows_k = rows_in[0].shape[0], key_in[0].shape[0]
    gain = out_gain.reshape(1, width)
    half = max(1, local_heads // 2)
    firsts = (0, half)
    flow = []

    def send(array, far, j):
        if far == 0 and j == 0:
            return array
        pairs = [(i, (i + far * MEMBERS) % count ^ j) for i in range(count)]
        if len(flow) >= DEPTH:
            array = after(array, flow[-DEPTH])
        flow.append(lax.ppermute(array, "ctx", pairs))
        return flow[-1]

    def spread(near, far_pieces, sign, *before):
        near, far_pieces = list(near), list(far_pieces)
        for n, (is_far, j) in enumerate(ORDER):
            ready = before if n == 6 else ()
            if not is_far:
                near[j] = send(after(near[j], *ready), 0, j)
                continue
            for far in range(1, groups):
                p = (far - 1) * MEMBERS + j
                far_pieces[p] = send(after(far_pieces[p], *ready), sign * far, j)
        return near + far_pieces

    def outward(first, *before):
        arrays = (after(key_in[0], *before),) + key_in[1:]
        far_pieces = pack(
            table, arrays, local_heads, first, half, VMEM if first == 0 else VMEM // 2
        )
        near = pack(table, arrays + rows_in, local_heads, first, half, VMEM // 2)
        return spread(near, list(far_pieces) * (groups - 1), 1)

    def attend(first, pieces, *before):
        pieces = [after(pieces[0], *before)] + pieces[1:]
        out = attention(table, gain, pieces, rows_k, local_heads, first, half)
        return out[0], out[1 : 1 + MEMBERS], out[1 + MEMBERS :]

    pieces0 = outward(firsts[0])
    pieces1 = outward(firsts[1])
    out0 = attend(firsts[0], pieces0)
    back0 = spread(out0[1], out0[2], -1)
    out1 = attend(firsts[1], pieces1, back0[MEMBERS])
    grads = unpack(
        table, (0, 1, 2, 3), back0, None, rows_q, rows_k, width, local_heads, firsts[0]
    )
    back1 = spread(out1[1], out1[2], -1, grads[0])
    gain_mine = jnp.concatenate([out0[0], out1[0]]).reshape(groups, width // count)
    gain_mine = lax.psum(gain_mine, "dp")
    gain_grad = 0.0
    for far in range(groups):
        whose = lax.rem(group + far, groups)
        piece = lax.dynamic_slice_in_dim(gain_mine, whose, 1)[0]
        pairs = [
            (g * MEMBERS + r, r * groups + (g + far) % groups)
            for g in range(groups)
            for r in range(MEMBERS)
        ]
        gain_grad = gain_grad + lax.ppermute(after(piece, flow[-6]), "ctx", pairs)
    for chosen in ((0, 1, 3), (2,)):
        grads = unpack(
            table, chosen, back1, grads, rows_q, rows_k, width, local_heads, firsts[1]
        )
    return tuple(g[None] for g in tuple(grads[4:]) + tuple(grads[:4])) + (gain_grad,)


def solution(mesh):
    tokens = P("dp", "ctx", None)
    return jax.shard_map(
        per_device,
        mesh=mesh,
        in_specs=(tokens,) * 6 + (P(),) + (tokens,) * 2,
        out_specs=(tokens,) * 6 + (P("ctx"),),
        check_vma=False,
    )
```

```python
import functools
import math

import jax
import jax.numpy as jnp
from jax import lax
from jax.experimental import pallas as pl
from jax.experimental.pallas import tpu as pltpu
from jax.sharding import PartitionSpec as P

HEAD_DIM = 128
MEMBERS = 4
DEPTH = 5
ORDER = ((True, 0), (False, 3), (True, 1), (False, 2), (True, 3), (False, 1), (True, 2))
VMEM = 60 * 1024 * 1024
F32 = jnp.float32
BF16 = jnp.bfloat16


def dot(left, right, left_dim, right_dim):
    return lax.dot_general(
        left, right, (((left_dim,), (right_dim,)), ((), ())), preferred_element_type=F32
    )


def pack_kernel(groups_of_refs, table_ref, *refs):
    ins, outs = refs[: -MEMBERS], refs[-MEMBERS:]
    each = 4 * groups_of_refs
    for j, out_ref in enumerate(outs):
        for h in range(out_ref.shape[0]):
            row = 0
            for n, ref in enumerate(ins[each * j : each * (j + 1)]):
                i = n % 4
                out_ref[h, row : row + ref.shape[0], i * HEAD_DIM : (i + 1) * HEAD_DIM] = ref[
                    :, h * HEAD_DIM : (h + 1) * HEAD_DIM
                ]
                if i == 3:
                    row += ref.shape[0]


def pack(table, arrays, local_heads, first, count, vmem):
    rows = sum(a.shape[0] for a in arrays) // 4
    block = math.gcd(count, first, 2)
    steps = count // block

    def columns(array, j):
        return pl.BlockSpec(
            (array.shape[0], block * HEAD_DIM),
            lambda i, table_ref: (0, (table_ref[j] * local_heads + first) // block + i),
        )

    return pl.pallas_call(
        functools.partial(pack_kernel, len(arrays) // 4),
        grid_spec=pltpu.PrefetchScalarGridSpec(
            num_scalar_prefetch=1,
            grid=(steps,),
            in_specs=[columns(a, j) for j in range(MEMBERS) for a in arrays],
            out_specs=[
                pl.BlockSpec((block, rows, 4 * HEAD_DIM), lambda i, table_ref: (i, 0, 0))
            ]
            * MEMBERS,
        ),
        out_shape=[jax.ShapeDtypeStruct((count, rows, 4 * HEAD_DIM), BF16)] * MEMBERS,
        compiler_params=pltpu.CompilerParams(vmem_limit_bytes=vmem),
        cost_estimate=pl.CostEstimate(
            flops=0, bytes_accessed=MEMBERS * count * rows * HEAD_DIM * 16, transcendentals=0
        ),
    )(table, *(list(arrays) * MEMBERS))


def unpack_kernel(members, pieces, table_ref, *refs):
    outs = refs[-6:]
    key_rows, half_rows = outs[0].shape[0], outs[4].shape[0] // 2
    d = HEAD_DIM
    for j in range(members):

        @pl.when(pl.program_id(0) == j)
        def _(j=j):
            near = refs[j]
            total = near[:, :key_rows].astype(F32)
            for p in range(members + j, pieces, members):
                total = total + refs[p][...].astype(F32)
            for h in range(total.shape[0]):
                columns = slice(h * d, (h + 1) * d)
                for i, ref in enumerate(outs[:4]):
                    ref[:, columns] = total[h, :, i * d : (i + 1) * d].astype(BF16)
                for i, ref in enumerate(outs[4:]):
                    ref[:half_rows, columns] = near[h, key_rows:, i * d : (i + 1) * d]
                    ref[half_rows:, columns] = near[h, key_rows:, (i + 2) * d : (i + 3) * d]


def unpack(table, chosen, pieces, before, rows_q, rows_k, width, local_heads, first):
    count, lanes = pieces[0].shape[0], 4 * HEAD_DIM
    old = list(before or ())
    pieces = [p for n, p in enumerate(pieces) if n % MEMBERS in chosen]
    table = jnp.stack([table[j] for j in chosen])
    rows_of = [rows_k] * 4 + [rows_q] * 2
    return pl.pallas_call(
        functools.partial(unpack_kernel, len(chosen), len(pieces)),
        grid_spec=pltpu.PrefetchScalarGridSpec(
            num_scalar_prefetch=1,
            grid=(len(chosen),),
            in_specs=[
                pl.BlockSpec((count, p.shape[1], lanes), lambda j, table_ref: (0, 0, 0))
                for p in pieces
            ]
            + [pl.BlockSpec(memory_space=pl.ANY)] * len(old),
            out_specs=[
                pl.BlockSpec(
                    (rows, count * HEAD_DIM),
                    lambda j, table_ref: (0, (table_ref[j] * local_heads + first) // count),
                )
                for rows in rows_of
            ],
        ),
        out_shape=[jax.ShapeDtypeStruct((rows, width), BF16) for rows in rows_of],
        input_output_aliases={1 + len(pieces) + i: i for i in range(len(old))},
        compiler_params=pltpu.CompilerParams(vmem_limit_bytes=VMEM // 2),
        cost_estimate=pl.CostEstimate(
            flops=0, bytes_accessed=count * rows_k * lanes * MEMBERS * 16, transcendentals=0
        ),
    )(table, *pieces, *old)


def attention_kernel(pieces, key_rows, scale, table_ref, gain_ref, *refs):
    near_refs, far_refs = refs[:MEMBERS], refs[MEMBERS:pieces]
    gain_out, key_outs = refs[pieces], refs[pieces + 1 :]
    d = HEAD_DIM
    part_rows = near_refs[0].shape[1] - key_rows
    every = jnp.concatenate(
        [ref[0, :key_rows] for ref in near_refs] + [ref[0] for ref in far_refs], axis=0
    )
    k, k_kt = every[:, :d], every[:, : 2 * d]
    v, v_vt = every[:, 2 * d : 3 * d], every[:, 2 * d :]
    gain = gain_ref[...].astype(F32)
    sums = None
    for start in range(0, MEMBERS, 2):
        rows = jnp.concatenate(
            [near_refs[start][0, key_rows:], near_refs[start + 1][0, key_rows:]], axis=0
        )
        q, qt = rows[:, :d], rows[:, d : 2 * d]
        gy = rows[:, 2 * d : 3 * d].astype(F32)
        gyt = rows[:, 3 * d :].astype(F32)
        go = (gy * gain).astype(BF16)
        got = (gyt * gain).astype(BF16)
        go_got = jnp.concatenate([go, got], axis=1)

        scores = dot(q, k, 1, 1) * scale
        scores_tan = dot(jnp.concatenate([qt, q], axis=1), k_kt, 1, 1) * scale
        d_probs = dot(go_got, v_vt, 1, 1)
        d_probs_tan = dot(got, v, 1, 1)
        top = jnp.max(scores, axis=-1, keepdims=True)
        raised = jnp.exp(scores - top)
        probs = raised * (1.0 / jnp.sum(raised, axis=-1, keepdims=True))
        offset = jnp.sum(probs * scores_tan, axis=-1, keepdims=True)
        centred = scores_tan - offset
        p_low = probs.astype(BF16)
        pt_low = (probs * centred).astype(BF16)
        inner = jnp.sum(probs * d_probs_tan, axis=-1, keepdims=True)
        dst_low = (probs * (d_probs_tan - inner)).astype(BF16)
        totals = d_probs + d_probs_tan * centred - inner * scores_tan
        ds = probs * (totals - jnp.sum(probs * totals, axis=-1, keepdims=True))
        ds_low = ds.astype(BF16)

        out_pair = dot(p_low, v_vt, 1, 0)
        attn_out = out_pair[:, :d].astype(BF16).astype(F32)
        attn_tan = (dot(pt_low, v, 1, 0) + out_pair[:, d:]).astype(BF16).astype(F32)
        gain_sum = jnp.sum(gy * attn_out + gyt * attn_tan, axis=0, keepdims=True)
        q_pair = dot(dst_low, k_kt, 1, 0)
        dq = scale * (dot(ds_low, k, 1, 0) + q_pair[:, d:])
        dqt = scale * q_pair[:, :d]
        both = jnp.concatenate([dq, dqt], axis=1).astype(BF16)
        for n in range(4):
            key_outs[start + n // 2][0, key_rows:, (n % 2) * 2 * d : (n % 2 + 1) * 2 * d] = both[
                n * part_rows // 2 : (n + 1) * part_rows // 2
            ]

        k_pair = dot(dst_low, rows[:, : 2 * d], 0, 0)
        v_pair = dot(p_low, go_got, 0, 0)
        terms = (
            dot(ds_low, q, 0, 0) + k_pair[:, d:],
            k_pair[:, :d],
            v_pair[:, :d] + dot(pt_low, got, 0, 0),
            v_pair[:, d:],
            gain_sum,
        )
        sums = terms if sums is None else tuple(a + b for a, b in zip(sums, terms))
    dk, dkt, dv, dvt, gain_sum = sums
    gain_out[0] = gain_sum
    for i, part in enumerate((scale * dk, scale * dkt, dv, dvt)):
        columns = slice(i * d, (i + 1) * d)
        for p, ref in enumerate(key_outs):
            ref[0, :key_rows, columns] = part[p * key_rows : (p + 1) * key_rows].astype(ref.dtype)


def attention(table, gain, pieces, key_rows, local_heads, first, count):
    d = HEAD_DIM
    part_rows = pieces[0].shape[1] - key_rows
    home_rows = [key_rows + part_rows // 2] * MEMBERS
    home_rows += [key_rows] * (len(pieces) - MEMBERS)

    def spec(rows_of, lanes):
        return pl.BlockSpec((1, rows_of, lanes), lambda h, table_ref: (h, 0, 0))

    pairs = count * MEMBERS * part_rows * len(pieces) * key_rows
    return pl.pallas_call(
        functools.partial(attention_kernel, len(pieces), key_rows, 1.0 / math.sqrt(d)),
        grid_spec=pltpu.PrefetchScalarGridSpec(
            num_scalar_prefetch=1,
            grid=(count,),
            in_specs=[
                pl.BlockSpec(
                    (1, d), lambda h, table_ref: (0, table_ref[0] * local_heads + first + h)
                )
            ]
            + [spec(p.shape[1], 4 * d) for p in pieces],
            out_specs=[spec(1, d)] + [spec(rows, 4 * d) for rows in home_rows],
        ),
        out_shape=[jax.ShapeDtypeStruct((count, 1, d), F32)]
        + [jax.ShapeDtypeStruct((count, rows, 4 * d), BF16) for rows in home_rows],
        compiler_params=pltpu.CompilerParams(vmem_limit_bytes=VMEM),
        cost_estimate=pl.CostEstimate(
            flops=pairs * 36 * d, bytes_accessed=pairs * 8, transcendentals=pairs
        ),
    )(table, gain, *pieces)


def after(array, *before):
    return lax.optimization_barrier((array,) + before)[0] if before else array


def per_device(
    queries, query_tangent, keys, key_tangent, values, value_tangent, out_gain, grad_y, grad_y_tan
):
    count = lax.axis_size("ctx")
    groups = count // MEMBERS
    width = queries.shape[2]
    local_heads = width // HEAD_DIM // MEMBERS
    place = lax.axis_index("ctx")
    member, group = lax.rem(place, MEMBERS), place // MEMBERS
    table = jnp.stack([member ^ j for j in range(MEMBERS)]).astype(jnp.int32)

    rows_in = (queries[0], query_tangent[0], grad_y[0], grad_y_tan[0])
    key_in = (keys[0], key_tangent[0], values[0], value_tangent[0])
    rows_q, rows_k = rows_in[0].shape[0], key_in[0].shape[0]
    gain = out_gain.reshape(1, width)
    half = max(1, local_heads // 2)
    firsts = (0, half)
    flow = []

    def send(array, far, j):
        if far == 0 and j == 0:
            return array
        pairs = [(i, (i + far * MEMBERS) % count ^ j) for i in range(count)]
        if len(flow) >= DEPTH:
            array = after(array, flow[-DEPTH])
        flow.append(lax.ppermute(array, "ctx", pairs))
        return flow[-1]

    def spread(near, far_pieces, sign, *before):
        near, far_pieces = list(near), list(far_pieces)
        for n, (is_far, j) in enumerate(ORDER):
            ready = before if n == 6 else ()
            if not is_far:
                near[j] = send(after(near[j], *ready), 0, j)
                continue
            for far in range(1, groups):
                p = (far - 1) * MEMBERS + j
                far_pieces[p] = send(after(far_pieces[p], *ready), sign * far, j)
        return near + far_pieces

    def outward(first, *before):
        arrays = (after(key_in[0], *before),) + key_in[1:]
        far_pieces = pack(
            table, arrays, local_heads, first, half, VMEM if first == 0 else VMEM // 2
        )
        near = pack(table, arrays + rows_in, local_heads, first, half, VMEM)
        return spread(near, list(far_pieces) * (groups - 1), 1)

    def attend(first, pieces, *before):
        pieces = [after(pieces[0], *before)] + pieces[1:]
        out = attention(table, gain, pieces, rows_k, local_heads, first, half)
        return out[0], out[1 : 1 + MEMBERS], out[1 + MEMBERS :]

    pieces0 = outward(firsts[0])
    pieces1 = outward(firsts[1])
    out0 = attend(firsts[0], pieces0)
    back0 = spread(out0[1], out0[2], -1)
    out1 = attend(firsts[1], pieces1, back0[MEMBERS])
    grads = unpack(
        table, (0, 1, 2, 3), back0, None, rows_q, rows_k, width, local_heads, firsts[0]
    )
    back1 = spread(out1[1], out1[2], -1, grads[0])
    gain_mine = jnp.concatenate([out0[0], out1[0]]).reshape(groups, width // count)
    gain_mine = lax.psum(gain_mine, "dp")
    gain_grad = 0.0
    for far in range(groups):
        whose = lax.rem(group + far, groups)
        piece = lax.dynamic_slice_in_dim(gain_mine, whose, 1)[0]
        pairs = [
            (g * MEMBERS + r, r * groups + (g + far) % groups)
            for g in range(groups)
            for r in range(MEMBERS)
        ]
        gain_grad = gain_grad + lax.ppermute(after(piece, flow[-6]), "ctx", pairs)
    for chosen in ((0, 1, 3), (2,)):
        grads = unpack(
            table, chosen, back1, grads, rows_q, rows_k, width, local_heads, firsts[1]
        )
    return tuple(g[None] for g in tuple(grads[4:]) + tuple(grads[:4])) + (gain_grad,)


def solution(mesh):
    tokens = P("dp", "ctx", None)
    return jax.shard_map(
        per_device,
        mesh=mesh,
        in_specs=(tokens,) * 6 + (P(),) + (tokens,) * 2,
        out_specs=(tokens,) * 6 + (P("ctx"),),
        check_vma=False,
    )
```

```python
import functools
import math

import jax
import jax.numpy as jnp
from jax import lax
from jax.experimental import pallas as pl
from jax.experimental.pallas import tpu as pltpu
from jax.sharding import PartitionSpec as P

HEAD_DIM = 128
MEMBERS = 4
DEPTH = 5
ORDER = ((True, 0), (False, 3), (True, 1), (False, 2), (True, 3), (False, 1), (True, 2))
VMEM = 60 * 1024 * 1024
F32 = jnp.float32
BF16 = jnp.bfloat16


def dot(left, right, left_dim, right_dim):
    return lax.dot_general(
        left, right, (((left_dim,), (right_dim,)), ((), ())), preferred_element_type=F32
    )


def pack_kernel(groups_of_refs, table_ref, *refs):
    ins, outs = refs[: -MEMBERS], refs[-MEMBERS:]
    each = 4 * groups_of_refs
    for j, out_ref in enumerate(outs):
        for h in range(out_ref.shape[0]):
            row = 0
            for n, ref in enumerate(ins[each * j : each * (j + 1)]):
                i = n % 4
                out_ref[h, row : row + ref.shape[0], i * HEAD_DIM : (i + 1) * HEAD_DIM] = ref[
                    :, h * HEAD_DIM : (h + 1) * HEAD_DIM
                ]
                if i == 3:
                    row += ref.shape[0]


def pack(table, arrays, local_heads, first, count, vmem):
    rows = sum(a.shape[0] for a in arrays) // 4
    block = math.gcd(count, first, 4)
    steps = count // block

    def columns(array, j):
        return pl.BlockSpec(
            (array.shape[0], block * HEAD_DIM),
            lambda i, table_ref: (0, (table_ref[j] * local_heads + first) // block + i),
        )

    return pl.pallas_call(
        functools.partial(pack_kernel, len(arrays) // 4),
        grid_spec=pltpu.PrefetchScalarGridSpec(
            num_scalar_prefetch=1,
            grid=(steps,),
            in_specs=[columns(a, j) for j in range(MEMBERS) for a in arrays],
            out_specs=[
                pl.BlockSpec((block, rows, 4 * HEAD_DIM), lambda i, table_ref: (i, 0, 0))
            ]
            * MEMBERS,
        ),
        out_shape=[jax.ShapeDtypeStruct((count, rows, 4 * HEAD_DIM), BF16)] * MEMBERS,
        compiler_params=pltpu.CompilerParams(vmem_limit_bytes=vmem),
        cost_estimate=pl.CostEstimate(
            flops=0, bytes_accessed=MEMBERS * count * rows * HEAD_DIM * 16, transcendentals=0
        ),
    )(table, *(list(arrays) * MEMBERS))


def unpack_kernel(members, pieces, table_ref, *refs):
    outs = refs[-6:]
    key_rows, half_rows = outs[0].shape[0], outs[4].shape[0] // 2
    d = HEAD_DIM
    for j in range(members):

        @pl.when(pl.program_id(0) == j)
        def _(j=j):
            near = refs[j]
            total = near[:, :key_rows].astype(F32)
            for p in range(members + j, pieces, members):
                total = total + refs[p][...].astype(F32)
            for h in range(total.shape[0]):
                columns = slice(h * d, (h + 1) * d)
                for i, ref in enumerate(outs[:4]):
                    ref[:, columns] = total[h, :, i * d : (i + 1) * d].astype(BF16)
                for i, ref in enumerate(outs[4:]):
                    ref[:half_rows, columns] = near[h, key_rows:, i * d : (i + 1) * d]
                    ref[half_rows:, columns] = near[h, key_rows:, (i + 2) * d : (i + 3) * d]


def unpack(table, chosen, pieces, before, rows_q, rows_k, width, local_heads, first):
    count, lanes = pieces[0].shape[0], 4 * HEAD_DIM
    old = list(before or ())
    pieces = [p for n, p in enumerate(pieces) if n % MEMBERS in chosen]
    table = jnp.stack([table[j] for j in chosen])
    rows_of = [rows_k] * 4 + [rows_q] * 2
    return pl.pallas_call(
        functools.partial(unpack_kernel, len(chosen), len(pieces)),
        grid_spec=pltpu.PrefetchScalarGridSpec(
            num_scalar_prefetch=1,
            grid=(len(chosen),),
            in_specs=[
                pl.BlockSpec((count, p.shape[1], lanes), lambda j, table_ref: (0, 0, 0))
                for p in pieces
            ]
            + [pl.BlockSpec(memory_space=pl.ANY)] * len(old),
            out_specs=[
                pl.BlockSpec(
                    (rows, count * HEAD_DIM),
                    lambda j, table_ref: (0, (table_ref[j] * local_heads + first) // count),
                )
                for rows in rows_of
            ],
        ),
        out_shape=[jax.ShapeDtypeStruct((rows, width), BF16) for rows in rows_of],
        input_output_aliases={1 + len(pieces) + i: i for i in range(len(old))},
        compiler_params=pltpu.CompilerParams(vmem_limit_bytes=VMEM // 2),
        cost_estimate=pl.CostEstimate(
            flops=0, bytes_accessed=count * rows_k * lanes * MEMBERS * 16, transcendentals=0
        ),
    )(table, *pieces, *old)


def attention_kernel(pieces, key_rows, scale, table_ref, gain_ref, *refs):
    near_refs, far_refs = refs[:MEMBERS], refs[MEMBERS:pieces]
    gain_out, key_outs = refs[pieces], refs[pieces + 1 :]
    d = HEAD_DIM
    part_rows = near_refs[0].shape[1] - key_rows
    every = jnp.concatenate(
        [ref[0, :key_rows] for ref in near_refs] + [ref[0] for ref in far_refs], axis=0
    )
    k, k_kt = every[:, :d], every[:, : 2 * d]
    v, v_vt = every[:, 2 * d : 3 * d], every[:, 2 * d :]
    gain = gain_ref[...].astype(F32)
    sums = None
    for start in range(0, MEMBERS, 2):
        rows = jnp.concatenate(
            [near_refs[start][0, key_rows:], near_refs[start + 1][0, key_rows:]], axis=0
        )
        q, qt = rows[:, :d], rows[:, d : 2 * d]
        gy = rows[:, 2 * d : 3 * d].astype(F32)
        gyt = rows[:, 3 * d :].astype(F32)
        go = (gy * gain).astype(BF16)
        got = (gyt * gain).astype(BF16)
        go_got = jnp.concatenate([go, got], axis=1)

        scores = dot(q, k, 1, 1) * scale
        scores_tan = dot(jnp.concatenate([qt, q], axis=1), k_kt, 1, 1) * scale
        d_probs = dot(go_got, v_vt, 1, 1)
        d_probs_tan = dot(got, v, 1, 1)
        top = jnp.max(scores, axis=-1, keepdims=True)
        raised = jnp.exp(scores - top)
        probs = raised * (1.0 / jnp.sum(raised, axis=-1, keepdims=True))
        offset = jnp.sum(probs * scores_tan, axis=-1, keepdims=True)
        centred = scores_tan - offset
        p_low = probs.astype(BF16)
        pt_low = (probs * centred).astype(BF16)
        inner = jnp.sum(probs * d_probs_tan, axis=-1, keepdims=True)
        dst_low = (probs * (d_probs_tan - inner)).astype(BF16)
        totals = d_probs + d_probs_tan * centred - inner * scores_tan
        ds = probs * (totals - jnp.sum(probs * totals, axis=-1, keepdims=True))
        ds_low = ds.astype(BF16)

        out_pair = dot(p_low, v_vt, 1, 0)
        attn_out = out_pair[:, :d].astype(BF16).astype(F32)
        attn_tan = (dot(pt_low, v, 1, 0) + out_pair[:, d:]).astype(BF16).astype(F32)
        gain_sum = jnp.sum(gy * attn_out + gyt * attn_tan, axis=0, keepdims=True)
        q_pair = dot(dst_low, k_kt, 1, 0)
        dq = scale * (dot(ds_low, k, 1, 0) + q_pair[:, d:])
        dqt = scale * q_pair[:, :d]
        both = jnp.concatenate([dq, dqt], axis=1).astype(BF16)
        for n in range(4):
            key_outs[start + n // 2][0, key_rows:, (n % 2) * 2 * d : (n % 2 + 1) * 2 * d] = both[
                n * part_rows // 2 : (n + 1) * part_rows // 2
            ]

        k_pair = dot(dst_low, rows[:, : 2 * d], 0, 0)
        v_pair = dot(p_low, go_got, 0, 0)
        terms = (
            dot(ds_low, q, 0, 0) + k_pair[:, d:],
            k_pair[:, :d],
            v_pair[:, :d] + dot(pt_low, got, 0, 0),
            v_pair[:, d:],
            gain_sum,
        )
        sums = terms if sums is None else tuple(a + b for a, b in zip(sums, terms))
    dk, dkt, dv, dvt, gain_sum = sums
    gain_out[0] = gain_sum
    for i, part in enumerate((scale * dk, scale * dkt, dv, dvt)):
        columns = slice(i * d, (i + 1) * d)
        for p, ref in enumerate(key_outs):
            ref[0, :key_rows, columns] = part[p * key_rows : (p + 1) * key_rows].astype(ref.dtype)


def attention(table, gain, pieces, key_rows, local_heads, first, count):
    d = HEAD_DIM
    part_rows = pieces[0].shape[1] - key_rows
    home_rows = [key_rows + part_rows // 2] * MEMBERS
    home_rows += [key_rows] * (len(pieces) - MEMBERS)

    def spec(rows_of, lanes):
        return pl.BlockSpec((1, rows_of, lanes), lambda h, table_ref: (h, 0, 0))

    pairs = count * MEMBERS * part_rows * len(pieces) * key_rows
    return pl.pallas_call(
        functools.partial(attention_kernel, len(pieces), key_rows, 1.0 / math.sqrt(d)),
        grid_spec=pltpu.PrefetchScalarGridSpec(
            num_scalar_prefetch=1,
            grid=(count,),
            in_specs=[
                pl.BlockSpec(
                    (1, d), lambda h, table_ref: (0, table_ref[0] * local_heads + first + h)
                )
            ]
            + [spec(p.shape[1], 4 * d) for p in pieces],
            out_specs=[spec(1, d)] + [spec(rows, 4 * d) for rows in home_rows],
        ),
        out_shape=[jax.ShapeDtypeStruct((count, 1, d), F32)]
        + [jax.ShapeDtypeStruct((count, rows, 4 * d), BF16) for rows in home_rows],
        compiler_params=pltpu.CompilerParams(vmem_limit_bytes=VMEM),
        cost_estimate=pl.CostEstimate(
            flops=pairs * 36 * d, bytes_accessed=pairs * 8, transcendentals=pairs
        ),
    )(table, gain, *pieces)


def after(array, *before):
    return lax.optimization_barrier((array,) + before)[0] if before else array


def per_device(
    queries, query_tangent, keys, key_tangent, values, value_tangent, out_gain, grad_y, grad_y_tan
):
    count = lax.axis_size("ctx")
    groups = count // MEMBERS
    width = queries.shape[2]
    local_heads = width // HEAD_DIM // MEMBERS
    place = lax.axis_index("ctx")
    member, group = lax.rem(place, MEMBERS), place // MEMBERS
    table = jnp.stack([member ^ j for j in range(MEMBERS)]).astype(jnp.int32)

    rows_in = (queries[0], query_tangent[0], grad_y[0], grad_y_tan[0])
    key_in = (keys[0], key_tangent[0], values[0], value_tangent[0])
    rows_q, rows_k = rows_in[0].shape[0], key_in[0].shape[0]
    gain = out_gain.reshape(1, width)
    half = max(1, local_heads // 2)
    firsts = (0, half)
    flow = []

    def send(array, far, j):
        if far == 0 and j == 0:
            return array
        pairs = [(i, (i + far * MEMBERS) % count ^ j) for i in range(count)]
        if len(flow) >= DEPTH:
            array = after(array, flow[-DEPTH])
        flow.append(lax.ppermute(array, "ctx", pairs))
        return flow[-1]

    def spread(near, far_pieces, sign, *before):
        near, far_pieces = list(near), list(far_pieces)
        for n, (is_far, j) in enumerate(ORDER):
            ready = before if n == 6 else ()
            if not is_far:
                near[j] = send(after(near[j], *ready), 0, j)
                continue
            for far in range(1, groups):
                p = (far - 1) * MEMBERS + j
                far_pieces[p] = send(after(far_pieces[p], *ready), sign * far, j)
        return near + far_pieces

    def outward(first, *before):
        arrays = (after(key_in[0], *before),) + key_in[1:]
        far_pieces = pack(
            table, arrays, local_heads, first, half, VMEM if first == 0 else VMEM // 2
        )
        near = pack(table, arrays + rows_in, local_heads, first, half, VMEM)
        return spread(near, list(far_pieces) * (groups - 1), 1)

    def attend(first, pieces, *before):
        pieces = [after(pieces[0], *before)] + pieces[1:]
        out = attention(table, gain, pieces, rows_k, local_heads, first, half)
        return out[0], out[1 : 1 + MEMBERS], out[1 + MEMBERS :]

    pieces0 = outward(firsts[0])
    pieces1 = outward(firsts[1])
    out0 = attend(firsts[0], pieces0)
    back0 = spread(out0[1], out0[2], -1)
    out1 = attend(firsts[1], pieces1, back0[MEMBERS])
    grads = unpack(
        table, (0, 1, 2, 3), back0, None, rows_q, rows_k, width, local_heads, firsts[0]
    )
    back1 = spread(out1[1], out1[2], -1, grads[0])
    gain_mine = jnp.concatenate([out0[0], out1[0]]).reshape(groups, width // count)
    gain_mine = lax.psum(gain_mine, "dp")
    gain_grad = 0.0
    for far in range(groups):
        whose = lax.rem(group + far, groups)
        piece = lax.dynamic_slice_in_dim(gain_mine, whose, 1)[0]
        pairs = [
            (g * MEMBERS + r, r * groups + (g + far) % groups)
            for g in range(groups)
            for r in range(MEMBERS)
        ]
        gain_grad = gain_grad + lax.ppermute(after(piece, flow[-6]), "ctx", pairs)
    for chosen in ((0, 1, 3), (2,)):
        grads = unpack(
            table, chosen, back1, grads, rows_q, rows_k, width, local_heads, firsts[1]
        )
    return tuple(g[None] for g in tuple(grads[4:]) + tuple(grads[:4])) + (gain_grad,)


def solution(mesh):
    tokens = P("dp", "ctx", None)
    return jax.shard_map(
        per_device,
        mesh=mesh,
        in_specs=(tokens,) * 6 + (P(),) + (tokens,) * 2,
        out_specs=(tokens,) * 6 + (P("ctx"),),
        check_vma=False,
    )
```
